512 devices in a mesh: pair: 16 (over z_lo, core), aux: 32 (over y, z_hi, x).
Axes of the slice: x: 4, y: 4, z: 16 (z_hi: 2, z_lo: 8; z = z_hi * 8 + z_lo), core: 2. Of those that a mesh axis runs over, the one named last changes fastest.
Arguments:
- integral_strips: bfloat16 [32, 512, 20480], P('pair', None, 'aux'), may hold values from -6 to 6
- slot_row_block: int32 [32], replicated, may hold values from 0 to 47
- slot_strip_index: int32 [32], replicated, may hold values from 0 to 31
- slot_column_block: int32 [32], replicated, may hold values from 0 to 47
- block_live: int32 [32], replicated, may hold values from 0 to 1, as said below
- ao_factor: bfloat16 [6144, 4096], P('pair', 'aux'), may hold values from -6 to 6
- aux_factor: bfloat16 [4096, 20480], P('pair', 'aux'), may hold values from -0.00390625 to 0.00390625
Outputs:
- contraction: float32 [6144, 4096], P('pair', 'aux')
The draws below stay inside these ranges and needn't reach their ends.
Inputs may be any that keep to these rules, and one draw needn't show every extreme that they name: `block_live`: 1 marks a slot that survives screening; slots k of one index i of the pair axis are i * 2 to (i + 1) * 2 - 1; every index has 1 to 2 live slots, and some index has all 2 live.
All inputs are finite; a program needn't handle non-finite values.
Results may differ from the reference program's by a relative error of at most 0.0003.
Values may be sent and summed in bfloat16 or wider, within the bound.
A program may use at most 64 MiB of HBM per device.

```python
import jax
import jax.numpy as jnp
from jax import lax

BLOCK_FUNCTIONS = 128
STRIP_HEIGHT = 4
NAO = 6144
AUXILIARY_COUNT = 20480
RANK = 4096
SLOTS = 2
BLOCK_COUNT = 48
SLOT_TOTAL = 32
N_PAIR = 16


def draw_block_live(key, part):
    key = jax.random.fold_in(key, 7)
    key_count, key_full, key_turn = jax.random.split(key, 3)
    counts = jax.random.randint(key_count, (N_PAIR,), 1, SLOTS + 1)
    full_index = jax.random.randint(key_full, (), 0, N_PAIR)
    counts = jnp.where(jnp.arange(N_PAIR) == full_index, SLOTS, counts)
    rotation = jax.random.randint(key_turn, (N_PAIR, 1), 0, SLOTS)
    position = (jnp.arange(SLOTS)[None, :] + rotation) % SLOTS
    return (position < counts[:, None]).astype(jnp.int32).reshape(-1)


def touch_ends(drawn, own_key, smallest, high):
    place = [jax.random.randint(jax.random.fold_in(own_key, axis), (), 0, length) for axis, length in enumerate(drawn.shape)]
    longest = drawn.shape.index(max(drawn.shape))
    next_to = place[:longest] + [(place[longest] + 1) % drawn.shape[longest]] + place[longest + 1:]
    return drawn.at[tuple(place)].set(smallest).at[tuple(next_to)].set(high)


def level_of(rng, extent, pieces, low, largest):
    def one(dim, blocks):
        steps = jax.random.uniform(jax.random.fold_in(jax.random.fold_in(rng, 6), dim), (blocks,), jnp.float32, low / len(pieces), largest / len(pieces))
        return jnp.repeat(jnp.exp(steps), extent[dim] // blocks).reshape((-1,) + (1,) * (len(extent) - dim - 1))

    factor_of = one(*pieces[0])
    for cut in pieces[1:]:
        factor_of = factor_of * one(*cut)
    return factor_of


def centred(stream_key, shape, scale, most, cuts=(), held_as=jnp.bfloat16):
    factor_of = level_of(stream_key, shape, cuts, -0.22, 0.18) if cuts else 1.0
    drawn = jax.random.normal(stream_key, shape, jnp.float32) * scale * factor_of
    return jnp.minimum(jnp.maximum(drawn, -most), most).astype(held_as)


def setup_inputs(seed: int = 0) -> dict:
    arg_keys = jax.random.split(jax.random.key(seed), 8)
    return {
        "integral_strips": centred(arg_keys[0], (SLOT_TOTAL, STRIP_HEIGHT * BLOCK_FUNCTIONS, AUXILIARY_COUNT), 1.0, 6.0, ((0, 16), (2, 32))),
        "slot_row_block": touch_ends(jax.random.randint(arg_keys[1], (SLOT_TOTAL,), 0, BLOCK_COUNT), jax.random.fold_in(arg_keys[1], 1), 0, BLOCK_COUNT - 1).astype(jnp.int32),
        "slot_strip_index": touch_ends(jax.random.randint(arg_keys[2], (SLOT_TOTAL,), 0, BLOCK_FUNCTIONS // STRIP_HEIGHT), jax.random.fold_in(arg_keys[2], 1), 0, (BLOCK_FUNCTIONS // STRIP_HEIGHT) - 1).astype(jnp.int32),
        "slot_column_block": touch_ends(jax.random.randint(arg_keys[3], (SLOT_TOTAL,), 0, BLOCK_COUNT), jax.random.fold_in(arg_keys[3], 1), 0, BLOCK_COUNT - 1).astype(jnp.int32),
        "block_live": draw_block_live(jax.random.fold_in(arg_keys[7], 71), 0),
        "ao_factor": centred(arg_keys[5], (NAO, RANK), 1.0, 6.0, ((0, 16), (1, 32))),
        "aux_factor": centred(arg_keys[6], (RANK, AUXILIARY_COUNT), (BLOCK_FUNCTIONS * AUXILIARY_COUNT) ** -0.5, 0.00390625, ((0, 16), (1, 32))),
    }


def reference(integral_strips, slot_row_block, slot_strip_index, slot_column_block, block_live, ao_factor, aux_factor):
    block_total = NAO // BLOCK_FUNCTIONS
    strip_count = BLOCK_FUNCTIONS // STRIP_HEIGHT
    x_blocks = ao_factor.reshape(block_total, BLOCK_FUNCTIONS, RANK)

    def add_block(accumulated, index_k):
        row_block = slot_row_block[index_k]
        strip_here = slot_strip_index[index_k]
        col_block = slot_column_block[index_k]
        alive_flag = block_live[index_k].astype(jnp.float32)
        products = lax.dot_general(integral_strips[index_k], aux_factor, (((1,), (1,)), ((), ())), preferred_element_type=jnp.float32)
        x_rows = x_blocks[col_block].astype(jnp.float32)
        contrib = jnp.sum(products.reshape(STRIP_HEIGHT, BLOCK_FUNCTIONS, RANK) * x_rows[None], axis=1) * alive_flag
        return accumulated.at[row_block, strip_here].add(contrib), None

    start_value = jnp.zeros((block_total, strip_count, STRIP_HEIGHT, RANK), jnp.float32)
    indices = jnp.arange(N_PAIR * SLOTS).astype(jnp.int32)
    accumulated = lax.scan(add_block, start_value, indices)[0]
    return accumulated.reshape(NAO, RANK)
```

```python
import functools

import jax
import jax.numpy as jnp
from jax import lax
from jax.experimental import pallas as pl
from jax.experimental.pallas import tpu as pltpu
from jax.sharding import PartitionSpec as P

BLOCK_FUNCTIONS = 128
CORES = 2
HALVES = 2
ROW = 4
PIECES = 2
MESH = pl.DeviceIdType.MESH


def exchange_kernel(
    cols_ref,
    live_ref,
    ints_hbm,
    x_hbm,
    z_hbm,
    out_ref,
    zbuf,
    ibuf,
    xchip,
    xin,
    xout,
    xfull,
    tpart,
    trecv,
    sbuf,
    t2recv,
    fbuf,
    fin,
    local_sem,
    z_send,
    z_side,
    z_recv,
    xchip_send,
    xchip_recv,
    xr_send,
    xr_recv,
    xpeer_send,
    xpeer_recv,
    xg_send,
    xg_recv,
    t1_send,
    t1_recv,
    t2_send,
    t2_recv,
    t3_send,
    t3_recv,
):
    pairs = lax.axis_size("pair")
    auxes = lax.axis_size("aux")
    nz = pairs // CORES
    ny = auxes // (HALVES * ROW)
    plane = ny * ROW
    p = lax.axis_index("pair")
    j = lax.axis_index("aux")
    k = p // CORES
    c = p % CORES
    sib = p + 1 - 2 * c
    x = j % ROW
    half = (j // ROW) % HALVES
    y = j // (ROW * HALVES)
    peer = j + (1 - 2 * half) * ROW
    slots = ints_hbm.shape[0]
    blocks_own = x_hbm.shape[0]
    shard_rows = z_hbm.shape[0]
    piece_rows = shard_rows // PIECES
    chunks = shard_rows // BLOCK_FUNCTIONS
    width = BLOCK_FUNCTIONS
    mus = ints_hbm.shape[1] // width
    blocks_chip = CORES * blocks_own

    def aux_of(yy, hh, xx):
        return (yy * HALVES + hh) * ROW + xx

    def plane_aux(rel):
        return aux_of(lax.rem(y + rel // ROW, ny), half, lax.rem(x + rel % ROW, ROW))

    barrier = pltpu.get_barrier_semaphore()

    def greet_line(rel, _):
        pl.semaphore_signal(
            barrier, inc=1, device_id=(lax.rem(p + rel, pairs), j), device_id_type=MESH
        )
        return 0

    lax.fori_loop(1, pairs, greet_line, 0)

    def greet_plane(rel, _):
        pl.semaphore_signal(barrier, inc=1, device_id=(p, plane_aux(rel)), device_id_type=MESH)
        return 0

    lax.fori_loop(1, plane, greet_plane, 0)
    pl.semaphore_signal(barrier, inc=1, device_id=(p, peer), device_id_type=MESH)

    load_i = pltpu.make_async_copy(ints_hbm, ibuf, local_sem.at[0])
    load_z = pltpu.make_async_copy(z_hbm, zbuf.at[p], local_sem.at[1])
    own_x = xchip.at[pl.ds(c * blocks_own, blocks_own)]
    load_x = pltpu.make_async_copy(x_hbm, own_x, local_sem.at[2])
    load_x.start()
    load_z.start()
    load_i.start()
    pl.semaphore_wait(barrier, pairs - 1 + plane - 1 + 1)

    def z_copy(direction, shard_chip, piece, own=False):
        rows = pl.ds(piece * piece_rows, piece_rows)
        shard = shard_chip * CORES + c
        src = z_hbm.at[rows] if own else zbuf.at[shard, rows]
        target = p + CORES if direction == 0 else p - CORES
        return pltpu.make_async_remote_copy(
            src_ref=src,
            dst_ref=zbuf.at[shard, rows],
            send_sem=z_send.at[direction, shard_chip, piece],
            recv_sem=z_recv.at[shard, piece],
            device_id=(target, j),
            device_id_type=MESH,
        )

    def z_side_copy(shard_chip, piece, own=False):
        rows = pl.ds(piece * piece_rows, piece_rows)
        shard = shard_chip * CORES + c
        src = z_hbm.at[rows] if own else zbuf.at[shard, rows]
        return pltpu.make_async_remote_copy(
            src_ref=src,
            dst_ref=zbuf.at[shard, rows],
            send_sem=z_side.at[0],
            recv_sem=z_recv.at[shard, piece],
            device_id=(sib, j),
            device_id_type=MESH,
        )

    def z_arrived(shard, piece):
        rows = pl.ds(piece * piece_rows, piece_rows)
        pltpu.make_async_copy(
            zbuf.at[shard, rows], zbuf.at[shard, rows], z_recv.at[shard, piece]
        ).wait()

    x_side = pltpu.make_async_remote_copy(
        src_ref=x_hbm,
        dst_ref=own_x,
        send_sem=xchip_send.at[0],
        recv_sem=xchip_recv.at[0],
        device_id=(sib, j),
        device_id_type=MESH,
    )
    x_side.start()
    for piece in range(PIECES):

        @pl.when(k < nz - 1)
        def _():
            z_copy(0, k, piece, own=True).start()

        @pl.when(k > 0)
        def _():
            z_copy(1, k, piece, own=True).start()

    for piece in range(PIECES):
        z_side_copy(k, piece, own=True).start()

    load_x.wait()
    pltpu.make_async_copy(own_x, own_x, xchip_recv.at[0]).wait()

    def picked(dest, slot):
        number = (dest * CORES + c) * slots + slot
        local = cols_ref[number] - k * blocks_chip
        near = jnp.minimum(jnp.maximum(local, 0), blocks_chip - 1)
        here = (near == local).astype(jnp.float32)
        return xchip[near].astype(jnp.float32) * here

    def x_copy(direction, dest):
        target = p + CORES if direction == 0 else p - CORES
        return pltpu.make_async_remote_copy(
            src_ref=xout.at[dest],
            dst_ref=xin.at[direction, dest],
            send_sem=xr_send.at[direction, dest],
            recv_sem=xr_recv.at[direction, dest],
            device_id=(target, j),
            device_id_type=MESH,
        )

    def x_arrived(direction, dest):
        pltpu.make_async_copy(
            xin.at[direction, dest], xin.at[direction, dest], xr_recv.at[direction, dest]
        ).wait()

    def x_step(tau, _):
        for direction in range(2):
            place = k if direction == 0 else nz - 1 - k
            far = nz - 1 - tau + place
            dest = far if direction == 0 else nz - 1 - far

            @pl.when(place <= tau)
            def _():
                @pl.when(place > 0)
                def _():
                    x_arrived(direction, dest)
                    for slot in range(slots):
                        got = xin[direction, dest, slot].astype(jnp.float32)
                        xout[dest, slot] = (picked(dest, slot) + got).astype(xout.dtype)

                @pl.when(place == 0)
                def _():
                    for slot in range(slots):
                        xout[dest, slot] = picked(dest, slot).astype(xout.dtype)

                x_copy(direction, dest).start()

        return 0

    lax.fori_loop(0, nz - 1, x_step, 0)

    for slot in range(slots):
        xout[k, slot] = picked(k, slot).astype(xout.dtype)

    @pl.when(k > 0)
    def _():
        x_arrived(0, k)
        for slot in range(slots):
            total = xout[k, slot].astype(jnp.float32) + xin[0, k, slot].astype(jnp.float32)
            xout[k, slot] = total.astype(xout.dtype)

    @pl.when(k < nz - 1)
    def _():
        x_arrived(1, k)
        for slot in range(slots):
            total = xout[k, slot].astype(jnp.float32) + xin[1, k, slot].astype(jnp.float32)
            xout[k, slot] = total.astype(xout.dtype)

    xfull[j] = xout[k]

    x_peer = pltpu.make_async_remote_copy(
        src_ref=xout.at[k],
        dst_ref=xfull.at[j],
        send_sem=xpeer_send.at[0],
        recv_sem=xpeer_recv.at[0],
        device_id=(p, peer),
        device_id_type=MESH,
    )
    x_peer.start()

    def x_plane(which):
        def body(rel, _):
            pltpu.make_async_remote_copy(
                src_ref=xfull.at[which],
                dst_ref=xfull.at[which],
                send_sem=xg_send.at[0],
                recv_sem=xg_recv.at[0],
                device_id=(p, plane_aux(rel)),
                device_id_type=MESH,
            ).start()
            return 0

        lax.fori_loop(1, plane, body, 0)

    x_plane(j)

    def contract(shard):
        z = zbuf[shard]
        for slot in range(slots):
            products = lax.dot_general(
                ibuf[slot], z, (((1,), (1,)), ((), ())), preferred_element_type=jnp.float32
            )
            alive = live_ref[p * slots + slot].astype(jnp.float32)
            for h in range(chunks):
                chunk = shard * chunks + h
                rows = xfull[chunk, slot].astype(jnp.float32)
                part = products[:, h * width : (h + 1) * width].reshape(mus, width, width)
                term = jnp.sum(part * rows[None], axis=1) * alive
                tpart[chunk, slot * mus : (slot + 1) * mus, :] = term
        for h in range(chunks):
            chunk = shard * chunks + h
            yy = chunk // (HALVES * ROW)
            hh = (chunk // ROW) % HALVES
            xx = chunk % ROW
            rel = lax.rem(y - yy + ny, ny) * ROW + lax.rem(x - xx + ROW, ROW)

            @pl.when(rel > 0)
            def _():
                pltpu.make_async_remote_copy(
                    src_ref=tpart.at[chunk],
                    dst_ref=trecv.at[rel - 1, hh],
                    send_sem=t1_send.at[0],
                    recv_sem=t1_recv.at[0],
                    device_id=(p, aux_of(yy, half, xx)),
                    device_id_type=MESH,
                ).start()

    def contract_set(step):
        def one(n, _):
            direction = n // CORES
            core = lax.rem(c + n, CORES)
            chip = jnp.where(direction == 0, k - step, k + step)
            shard = chip * CORES + core
            valid = jnp.logical_and(chip >= 0, chip < nz)
            valid = jnp.logical_and(valid, jnp.logical_or(step > 0, direction == 0))

            @pl.when(valid)
            def _():
                @pl.when(core != c)
                def _():
                    for piece in range(PIECES):
                        z_arrived(shard, piece)

                contract(shard)

            return 0

        lax.fori_loop(0, 2 * CORES, one, 0)

    load_z.wait()
    load_i.wait()

    first = nz // 2 + 1

    def z_step(t, _):
        for piece in range(PIECES):

            @pl.when(k - t >= 0)
            def _():
                z_arrived((k - t) * CORES + c, piece)

                @pl.when(k < nz - 1)
                def _():
                    z_copy(0, k - t, piece).start()

                z_side_copy(k - t, piece).start()

            @pl.when(k + t < nz)
            def _():
                z_arrived((k + t) * CORES + c, piece)

                @pl.when(k > 0)
                def _():
                    z_copy(1, k + t, piece).start()

                z_side_copy(k + t, piece).start()

        @pl.when(t == 1)
        def _():
            pltpu.make_async_copy(xfull.at[0], xfull.at[0], xpeer_recv.at[0]).wait()
            x_plane(peer)

        @pl.when(t == first)
        def _():
            everything = xfull.at[pl.ds(0, HALVES * (plane - 1))]
            pltpu.make_async_copy(everything, everything, xg_recv.at[0]).wait()

        @pl.when(t >= first)
        def _():
            contract_set(2 * (t - first))
            contract_set(2 * (t - first) + 1)

        return 0

    lax.fori_loop(1, 2 * first - 1, z_step, 0)

    pltpu.make_async_copy(trecv, trecv, t1_recv.at[0]).wait()
    mine = jnp.sum(trecv[:, half], axis=0) + tpart[aux_of(y, half, x)]
    theirs = jnp.sum(trecv[:, 1 - half], axis=0) + tpart[aux_of(y, 1 - half, x)]
    sbuf[...] = theirs
    t2 = pltpu.make_async_remote_copy(
        src_ref=sbuf,
        dst_ref=t2recv,
        send_sem=t2_send.at[0],
        recv_sem=t2_recv.at[0],
        device_id=(p, peer),
        device_id_type=MESH,
    )
    t2.start()
    t2.wait_recv()
    final = mine + t2recv[...]
    fbuf[...] = final
    out_ref[p] = final

    def spread(rel, _):
        pltpu.make_async_remote_copy(
            src_ref=fbuf,
            dst_ref=fin.at[pairs - 1 - rel],
            send_sem=t3_send.at[0],
            recv_sem=t3_recv.at[0],
            device_id=(lax.rem(p + rel, pairs), j),
            device_id_type=MESH,
        ).start()
        return 0

    lax.fori_loop(1, pairs, spread, 0)
    pltpu.make_async_copy(fin, fin, t3_recv.at[0]).wait()

    def take(rel, _):
        out_ref[lax.rem(p + rel, pairs)] = fin[rel - 1]
        return 0

    lax.fori_loop(1, pairs, take, 0)

    x_side.wait_send()
    x_peer.wait_send()
    t2.wait_send()
    pltpu.make_async_copy(fin, fin, t3_send.at[0]).wait()
    pltpu.make_async_copy(trecv, trecv, t1_send.at[0]).wait()
    sent = xfull.at[pl.ds(0, HALVES * (plane - 1))]
    pltpu.make_async_copy(sent, sent, xg_send.at[0]).wait()
    sent_z = zbuf.at[pl.ds(0, nz)]
    pltpu.make_async_copy(sent_z, sent_z, z_side.at[0]).wait()

    def z_sent(chip, _):
        @pl.when(jnp.logical_and(chip <= k, k < nz - 1))
        def _():
            for piece in range(PIECES):
                z_copy(0, chip, piece).wait_send()

        @pl.when(jnp.logical_and(chip >= k, k > 0))
        def _():
            for piece in range(PIECES):
                z_copy(1, chip, piece).wait_send()

        @pl.when(chip > k)
        def _():
            x_copy(0, chip).wait_send()

        @pl.when(chip < k)
        def _():
            x_copy(1, chip).wait_send()

        return 0

    lax.fori_loop(0, nz, z_sent, 0)


def place_kernel(first_block, blocks_dev, strips, slots, rows_ref, strip_ref, sums_ref, out_ref):
    out_ref[...] = jnp.zeros_like(out_ref)
    base = first_block[0]
    rows, columns = sums_ref.shape[1:]
    mus = rows // slots
    sublane = lax.broadcasted_iota(jnp.int32, (rows, columns), 0) // mus

    def body(p, _):
        value = sums_ref[p]
        turned = pltpu.roll(value, mus, 0)
        for slot in range(slots):
            number = p * slots + slot
            local = rows_ref[number] - base
            strip = local * strips + strip_ref[number]
            part = strip % slots
            tile = strip // slots

            @pl.when(jnp.logical_and(local >= 0, local < blocks_dev))
            def _():
                moved = jnp.where(part == slot, value, turned)
                kept = jnp.where(sublane == part, moved, 0.0)
                at = pl.ds(pl.multiple_of(tile * rows, rows), rows)
                out_ref[at, :] = out_ref[at, :] + kept

        return 0

    lax.fori_loop(0, sums_ref.shape[0], body, 0)


def per_device(
    integral_strips,
    slot_row_block,
    slot_strip_index,
    slot_column_block,
    block_live,
    ao_factor,
    aux_factor,
):
    slots, strip_size, depth = integral_strips.shape
    width = BLOCK_FUNCTIONS
    mus = strip_size // width
    pairs = lax.axis_size("pair")
    auxes = lax.axis_size("aux")
    nz = pairs // CORES
    plane = auxes // HALVES
    shard_rows = aux_factor.shape[0]
    rows_x, rank_part = ao_factor.shape
    blocks_dev = rows_x // width
    x_blocks = ao_factor.reshape(blocks_dev, width, rank_part)
    smem = pl.BlockSpec(memory_space=pltpu.SMEM)
    hbm = pl.BlockSpec(memory_space=pl.ANY)
    vmem = pl.BlockSpec(memory_space=pltpu.VMEM)
    rows = slots * mus
    dma = pltpu.SemaphoreType.DMA
    sums = pl.pallas_call(
        exchange_kernel,
        out_shape=jax.ShapeDtypeStruct((pairs, rows, rank_part), jnp.float32),
        in_specs=[smem, smem, hbm, hbm, hbm],
        out_specs=vmem,
        scratch_shapes=[
            pltpu.VMEM((pairs, shard_rows, depth), jnp.bfloat16),
            pltpu.VMEM((slots, strip_size, depth), jnp.bfloat16),
            pltpu.VMEM((CORES * blocks_dev, width, rank_part), jnp.bfloat16),
            pltpu.VMEM((2, nz, slots, width, rank_part), jnp.bfloat16),
            pltpu.VMEM((nz, slots, width, rank_part), jnp.bfloat16),
            pltpu.VMEM((auxes, slots, width, rank_part), jnp.bfloat16),
            pltpu.VMEM((auxes, rows, rank_part), jnp.float32),
            pltpu.VMEM((plane - 1, HALVES, rows, rank_part), jnp.float32),
            pltpu.VMEM((rows, rank_part), jnp.float32),
            pltpu.VMEM((rows, rank_part), jnp.float32),
            pltpu.VMEM((rows, rank_part), jnp.float32),
            pltpu.VMEM((pairs - 1, rows, rank_part), jnp.float32),
            dma((3,)),
            dma((2, nz, PIECES)),
            dma((1,)),
            dma((pairs, PIECES)),
            dma((1,)),
            dma((1,)),
            dma((2, nz)),
            dma((2, nz)),
            dma((1,)),
            dma((1,)),
            dma((1,)),
            dma((1,)),
            dma((1,)),
            dma((1,)),
            dma((1,)),
            dma((1,)),
            dma((1,)),
            dma((1,)),
        ],
        compiler_params=pltpu.CompilerParams(
            collective_id=0, has_side_effects=True, vmem_limit_bytes=40 * 2**20
        ),
        name="exchange",
    )(slot_column_block, block_live, integral_strips, x_blocks, aux_factor)

    first_block = (lax.axis_index("pair") * blocks_dev).astype(jnp.int32).reshape(1)
    return pl.pallas_call(
        lambda base, *refs: place_kernel(base, blocks_dev, width // mus, slots, *refs),
        out_shape=jax.ShapeDtypeStruct((rows_x, rank_part), jnp.float32),
        in_specs=[smem, smem, smem, vmem],
        out_specs=vmem,
        name="place",
    )(first_block, slot_row_block, slot_strip_index, sums)


def solution(mesh):
    in_specs = (P("pair", None, "aux"), P(), P(), P(), P(), P("pair", "aux"), P("pair", "aux"))
    out_specs = P("pair", "aux")
    return jax.shard_map(
        per_device, mesh=mesh, in_specs=in_specs, out_specs=out_specs, check_vma=False
    )
```

```python
import functools

import jax
import jax.numpy as jnp
from jax import lax
from jax.experimental import pallas as pl
from jax.experimental.pallas import tpu as pltpu
from jax.sharding import PartitionSpec as P

BLOCK_FUNCTIONS = 128
CORES = 2
HALVES = 2
ROW = 4
PIECES = 2
LEAD = 3
EVENTS = {8: (11, 11, 11, 12, 12, 12, 12, 13), 4: (1, 2, 3, 5), 2: (1, 1)}
PEER_LAG = 6
MESH = pl.DeviceIdType.MESH


def exchange_kernel(
    cols_hbm,
    live_hbm,
    ints_hbm,
    x_hbm,
    z_hbm,
    out_ref,
    cols_ref,
    live_ref,
    zbuf,
    ibuf,
    xchip,
    xin,
    xout,
    xfull,
    tpart,
    trecv,
    sbuf,
    fin,
    local_sem,
    z_send,
    z_side,
    z_recv,
    xchip_send,
    xchip_recv,
    xr_send,
    xr_recv,
    xpeer_send,
    xpeer_recv,
    xg_send,
    xg_recv,
    t1_send,
    t1_recv,
    t2_send,
    t2_recv,
):
    pairs = lax.axis_size("pair")
    auxes = lax.axis_size("aux")
    nz = pairs // CORES
    ny = auxes // (HALVES * ROW)
    plane = ny * ROW
    p = lax.axis_index("pair")
    j = lax.axis_index("aux")
    k = p // CORES
    c = p % CORES
    sib = p + 1 - 2 * c
    x = j % ROW
    half = (j // ROW) % HALVES
    y = j // (ROW * HALVES)
    peer = j + (1 - 2 * half) * ROW
    slots = ints_hbm.shape[0]
    blocks_own = x_hbm.shape[0]
    shard_rows = z_hbm.shape[0]
    piece_rows = shard_rows // PIECES
    chunks = shard_rows // BLOCK_FUNCTIONS
    width = BLOCK_FUNCTIONS
    mus = ints_hbm.shape[1] // width
    blocks_chip = CORES * blocks_own

    def aux_of(yy, hh, xx):
        return (yy * HALVES + hh) * ROW + xx

    def plane_aux(rel):
        return aux_of(lax.rem(y + rel // ROW, ny), half, lax.rem(x + rel % ROW, ROW))

    barrier = pltpu.get_barrier_semaphore()

    def greet_line(rel, _):
        pl.semaphore_signal(
            barrier, inc=1, device_id=(lax.rem(p + rel, pairs), j), device_id_type=MESH
        )
        return 0

    lax.fori_loop(1, pairs, greet_line, 0)

    def greet_plane(rel, _):
        pl.semaphore_signal(barrier, inc=1, device_id=(p, plane_aux(rel)), device_id_type=MESH)
        return 0

    lax.fori_loop(1, plane, greet_plane, 0)

    def greet_peers(rel, _):
        pl.semaphore_signal(
            barrier, inc=1, device_id=(lax.rem(p + rel, pairs), peer), device_id_type=MESH
        )
        return 0

    lax.fori_loop(0, pairs, greet_peers, 0)

    load_i = pltpu.make_async_copy(ints_hbm, ibuf, local_sem.at[0])
    load_z = pltpu.make_async_copy(z_hbm, zbuf.at[p], local_sem.at[1])
    own_x = xchip.at[pl.ds(c * blocks_own, blocks_own)]
    load_x = pltpu.make_async_copy(x_hbm, own_x, local_sem.at[2])
    load_cols = pltpu.make_async_copy(cols_hbm, cols_ref, local_sem.at[3])
    load_live = pltpu.make_async_copy(live_hbm, live_ref, local_sem.at[4])
    load_x.start()
    load_cols.start()
    load_live.start()
    load_z.start()
    load_i.start()
    pl.semaphore_wait(barrier, 2 * pairs - 1 + plane - 1)

    def z_copy(direction, shard_chip, piece, own=False):
        rows = pl.ds(pl.multiple_of(piece * piece_rows, piece_rows), piece_rows)
        shard = shard_chip * CORES + c
        src = z_hbm.at[rows] if own else zbuf.at[shard, rows]
        target = p + CORES if direction == 0 else p - CORES
        return pltpu.make_async_remote_copy(
            src_ref=src,
            dst_ref=zbuf.at[shard, rows],
            send_sem=z_send.at[direction, shard_chip, piece],
            recv_sem=z_recv.at[shard, piece],
            device_id=(target, j),
            device_id_type=MESH,
        )

    def z_side_copy(shard_chip, piece, own=False):
        rows = pl.ds(pl.multiple_of(piece * piece_rows, piece_rows), piece_rows)
        shard = shard_chip * CORES + c
        src = z_hbm.at[rows] if own else zbuf.at[shard, rows]
        return pltpu.make_async_remote_copy(
            src_ref=src,
            dst_ref=zbuf.at[shard, rows],
            send_sem=z_side.at[0],
            recv_sem=z_recv.at[shard, piece],
            device_id=(sib, j),
            device_id_type=MESH,
        )

    def z_arrived(shard, piece):
        rows = pl.ds(pl.multiple_of(piece * piece_rows, piece_rows), piece_rows)
        pltpu.make_async_copy(
            zbuf.at[shard, rows], zbuf.at[shard, rows], z_recv.at[shard, piece]
        ).wait()

    x_side = pltpu.make_async_remote_copy(
        src_ref=x_hbm,
        dst_ref=own_x,
        send_sem=xchip_send.at[0],
        recv_sem=xchip_recv.at[0],
        device_id=(sib, j),
        device_id_type=MESH,
    )
    x_side.start()
    for piece in range(PIECES):

        @pl.when(k < nz - 1)
        def _():
            z_copy(0, k, piece, own=True).start()

        @pl.when(k > 0)
        def _():
            z_copy(1, k, piece, own=True).start()

    for piece in range(PIECES):
        z_side_copy(k, piece, own=True).start()

    load_x.wait()
    load_cols.wait()
    load_live.wait()
    pltpu.make_async_copy(own_x, own_x, xchip_recv.at[0]).wait()

    def picked(dest, slot):
        number = (dest * CORES + c) * slots + slot
        local = cols_ref[number] - k * blocks_chip
        near = jnp.minimum(jnp.maximum(local, 0), blocks_chip - 1)
        here = (near == local).astype(jnp.float32)
        return xchip[near].astype(jnp.float32) * here

    def x_copy(direction, dest):
        target = p + CORES if direction == 0 else p - CORES
        return pltpu.make_async_remote_copy(
            src_ref=xout.at[dest],
            dst_ref=xin.at[direction, dest],
            send_sem=xr_send.at[direction, dest],
            recv_sem=xr_recv.at[direction, dest],
            device_id=(target, j),
            device_id_type=MESH,
        )

    def x_arrived(direction, dest):
        pltpu.make_async_copy(
            xin.at[direction, dest], xin.at[direction, dest], xr_recv.at[direction, dest]
        ).wait()

    def x_step(tau, _):
        for direction in range(2):
            place = k if direction == 0 else nz - 1 - k
            far = nz - 1 - tau + place
            dest = far if direction == 0 else nz - 1 - far

            @pl.when(place <= tau)
            def _():
                @pl.when(place > 0)
                def _():
                    x_arrived(direction, dest)
                    for slot in range(slots):
                        got = xin[direction, dest, slot].astype(jnp.float32)
                        xout[dest, slot] = (picked(dest, slot) + got).astype(xout.dtype)

                @pl.when(place == 0)
                def _():
                    for slot in range(slots):
                        xout[dest, slot] = picked(dest, slot).astype(xout.dtype)

                x_copy(direction, dest).start()

        return 0

    lead = min(LEAD, nz - 1)
    lax.fori_loop(0, lead, x_step, 0)

    x_peer = pltpu.make_async_remote_copy(
        src_ref=xout.at[k],
        dst_ref=xfull.at[j],
        send_sem=xpeer_send.at[0],
        recv_sem=xpeer_recv.at[0],
        device_id=(p, peer),
        device_id_type=MESH,
    )

    def x_last():
        for slot in range(slots):
            xout[k, slot] = picked(k, slot).astype(xout.dtype)

        @pl.when(k > 0)
        def _():
            x_arrived(0, k)
            for slot in range(slots):
                total = xout[k, slot].astype(jnp.float32) + xin[0, k, slot].astype(jnp.float32)
                xout[k, slot] = total.astype(xout.dtype)

        @pl.when(k < nz - 1)
        def _():
            x_arrived(1, k)
            for slot in range(slots):
                total = xout[k, slot].astype(jnp.float32) + xin[1, k, slot].astype(jnp.float32)
                xout[k, slot] = total.astype(xout.dtype)

        xfull[j] = xout[k]
        x_peer.start()

    def x_plane(which, which_half):
        def body(rel, _):
            pltpu.make_async_remote_copy(
                src_ref=xfull.at[which],
                dst_ref=xfull.at[which],
                send_sem=xg_send.at[which_half],
                recv_sem=xg_recv.at[which_half],
                device_id=(p, plane_aux(rel)),
                device_id_type=MESH,
            ).start()
            return 0

        lax.fori_loop(1, plane, body, 0)

    def x_plane_arrived(which_half):
        some = xfull.at[pl.ds(0, plane - 1)]
        pltpu.make_async_copy(some, some, xg_recv.at[which_half]).wait()

    def contract(shard):
        z = zbuf[shard]
        for slot in range(slots):
            products = lax.dot_general(
                ibuf[slot], z, (((1,), (1,)), ((), ())), preferred_element_type=jnp.float32
            )
            alive = live_ref[p * slots + slot].astype(jnp.float32)
            for h in range(chunks):
                chunk = shard * chunks + h
                rows = xfull[chunk, slot].astype(jnp.float32)
                part = products[:, h * width : (h + 1) * width].reshape(mus, width, width)
                term = jnp.sum(part * rows[None], axis=1) * alive
                tpart[chunk, slot * mus : (slot + 1) * mus, :] = term
        for h in range(chunks):
            chunk = shard * chunks + h
            yy = chunk // (HALVES * ROW)
            hh = (chunk // ROW) % HALVES
            xx = chunk % ROW
            rel = lax.rem(y - yy + ny, ny) * ROW + lax.rem(x - xx + ROW, ROW)

            @pl.when(rel > 0)
            def _():
                pltpu.make_async_remote_copy(
                    src_ref=tpart.at[chunk],
                    dst_ref=trecv.at[hh, rel - 1],
                    send_sem=t1_send.at[0],
                    recv_sem=t1_recv.at[hh],
                    device_id=(p, aux_of(yy, half, xx)),
                    device_id_type=MESH,
                ).start()

    def contract_set(step):
        def one(n, _):
            direction = n // CORES
            core = lax.rem(c + n, CORES)
            chip = jnp.where(direction == 0, k - step, k + step)
            shard = chip * CORES + core
            valid = jnp.logical_and(chip >= 0, chip < nz)
            valid = jnp.logical_and(valid, jnp.logical_or(step > 0, direction == 0))

            @pl.when(valid)
            def _():
                @pl.when(core != c)
                def _():
                    for piece in range(PIECES):
                        z_arrived(shard, piece)

                contract(shard)

            return 0

        lax.fori_loop(0, 2 * CORES, one, 0)

    load_z.wait()
    load_i.wait()

    done_at = EVENTS[nz]
    early = nz // 2 - 1
    own_parity = lax.rem(half + k, 2)

    def step_of(item):
        own = own_parity + 2 * item
        other = 1 - own_parity + 2 * (item - early)
        return jnp.where(item < early, own, jnp.where(item < 2 * early, other, item))

    def item_of(step):
        own = lax.rem(step + own_parity, 2) == 0
        listed = jnp.where(own, (step - own_parity) // 2, early + (step - 1 + own_parity) // 2)
        return jnp.where(step < 2 * early, listed, step)

    def finished_at(item):
        event = jnp.int32(done_at[0])
        for n in range(1, nz):
            event = jnp.where(item >= n, done_at[n], event)
        return event

    def items_by(event):
        count = jnp.int32(0)
        for n in range(nz):
            count = count + (event >= done_at[n]).astype(jnp.int32)
        return count

    last_event = 2 * (nz - 1)
    x_event = nz - 1 - lead
    peer_event = min(x_event + PEER_LAG, done_at[early])

    def spread(hh):
        pltpu.make_async_copy(trecv.at[hh], trecv.at[hh], t1_recv.at[hh]).wait()
        sbuf[hh] = jnp.sum(trecv[hh], axis=0) + tpart[aux_of(y, hh, x)]
        near = jnp.where(half == hh, 1, 0)

        def send(rel, _):
            slot = jnp.where(half == hh, pairs - 1 - rel, pairs - 1 + lax.rem(pairs - rel, pairs))
            pltpu.make_async_remote_copy(
                src_ref=sbuf.at[hh],
                dst_ref=fin.at[slot],
                send_sem=t2_send.at[0],
                recv_sem=t2_recv.at[0],
                device_id=(lax.rem(p + rel, pairs), aux_of(y, hh, x)),
                device_id_type=MESH,
            ).start()
            return 0

        lax.fori_loop(near, pairs, send, 0)

    def event_step(event, _):
        t = event // 2 + 1
        piece = lax.rem(event, 2)

        @pl.when(k - t >= 0)
        def _():
            z_arrived((k - t) * CORES + c, piece)

            @pl.when(k < nz - 1)
            def _():
                z_copy(0, k - t, piece).start()

            z_side_copy(k - t, piece).start()

        @pl.when(k + t < nz)
        def _():
            z_arrived((k + t) * CORES + c, piece)

            @pl.when(k > 0)
            def _():
                z_copy(1, k + t, piece).start()

            z_side_copy(k + t, piece).start()

        @pl.when(event < x_event)
        def _():
            x_step(event + lead, 0)

        @pl.when(event == x_event)
        def _():
            x_last()
            x_plane(j, 0)

        @pl.when(event == peer_event)
        def _():
            pltpu.make_async_copy(xfull.at[0], xfull.at[0], xpeer_recv.at[0]).wait()
            x_plane(peer, 1)

        @pl.when(event == done_at[0])
        def _():
            x_plane_arrived(0)

        @pl.when(event == done_at[early])
        def _():
            x_plane_arrived(1)

        for hh in range(HALVES):
            step = jnp.abs(k - aux_of(y, hh, x) // (chunks * CORES))

            @pl.when(event == finished_at(item_of(step)) + 1)
            def _():
                spread(hh)

        def work(item, _):
            contract_set(step_of(item))
            return 0

        lax.fori_loop(items_by(event - 1), items_by(event), work, 0)

        return 0

    lax.fori_loop(0, last_event + 1, event_step, 0)

    pltpu.make_async_copy(fin, fin, t2_recv.at[0]).wait()
    out_ref[p] = sbuf[half] + fin[pairs - 1]

    def take(rel, _):
        out_ref[lax.rem(p + rel, pairs)] = fin[rel - 1] + fin[pairs - 1 + rel]
        return 0

    lax.fori_loop(1, pairs, take, 0)

    x_side.wait_send()
    x_peer.wait_send()
    pltpu.make_async_copy(fin, fin, t2_send.at[0]).wait()
    pltpu.make_async_copy(trecv, trecv, t1_send.at[0]).wait()
    sent = xfull.at[pl.ds(0, plane - 1)]
    for which in range(HALVES):
        pltpu.make_async_copy(sent, sent, xg_send.at[which]).wait()
    sent_z = zbuf.at[pl.ds(0, nz)]
    pltpu.make_async_copy(sent_z, sent_z, z_side.at[0]).wait()

    def z_sent(chip, _):
        @pl.when(jnp.logical_and(chip <= k, k < nz - 1))
        def _():
            for piece in range(PIECES):
                z_copy(0, chip, piece).wait_send()

        @pl.when(jnp.logical_and(chip >= k, k > 0))
        def _():
            for piece in range(PIECES):
                z_copy(1, chip, piece).wait_send()

        @pl.when(chip > k)
        def _():
            x_copy(0, chip).wait_send()

        @pl.when(chip < k)
        def _():
            x_copy(1, chip).wait_send()

        return 0

    lax.fori_loop(0, nz, z_sent, 0)


def place_kernel(first_block, blocks_dev, strips, slots, rows_ref, strip_ref, sums_ref, out_ref):
    out_ref[...] = jnp.zeros_like(out_ref)
    base = first_block[0]
    rows, columns = sums_ref.shape[1:]
    mus = rows // slots
    sublane = lax.broadcasted_iota(jnp.int32, (rows, columns), 0) // mus

    def body(p, _):
        value = sums_ref[p]
        turned = pltpu.roll(value, mus, 0)
        for slot in range(slots):
            number = p * slots + slot
            local = rows_ref[number] - base
            strip = local * strips + strip_ref[number]
            part = strip % slots
            tile = strip // slots

            @pl.when(jnp.logical_and(local >= 0, local < blocks_dev))
            def _():
                moved = jnp.where(part == slot, value, turned)
                kept = jnp.where(sublane == part, moved, 0.0)
                at = pl.ds(pl.multiple_of(tile * rows, rows), rows)
                out_ref[at, :] = out_ref[at, :] + kept

        return 0

    lax.fori_loop(0, sums_ref.shape[0], body, 0)


def per_device(
    integral_strips,
    slot_row_block,
    slot_strip_index,
    slot_column_block,
    block_live,
    ao_factor,
    aux_factor,
):
    slots, strip_size, depth = integral_strips.shape
    width = BLOCK_FUNCTIONS
    mus = strip_size // width
    pairs = lax.axis_size("pair")
    auxes = lax.axis_size("aux")
    nz = pairs // CORES
    plane = auxes // HALVES
    shard_rows = aux_factor.shape[0]
    rows_x, rank_part = ao_factor.shape
    blocks_dev = rows_x // width
    x_blocks = ao_factor.reshape(blocks_dev, width, rank_part)
    smem = pl.BlockSpec(memory_space=pltpu.SMEM)
    hbm = pl.BlockSpec(memory_space=pltpu.HBM)
    vmem = pl.BlockSpec(memory_space=pltpu.VMEM)
    rows = slots * mus
    dma = pltpu.SemaphoreType.DMA
    sums = pl.pallas_call(
        exchange_kernel,
        out_shape=jax.ShapeDtypeStruct((pairs, rows, rank_part), jnp.float32),
        in_specs=[hbm, hbm, hbm, hbm, hbm],
        out_specs=vmem,
        scratch_shapes=[
            pltpu.SMEM((slot_column_block.shape[0],), jnp.int32),
            pltpu.SMEM((block_live.shape[0],), jnp.int32),
            pltpu.VMEM((pairs, shard_rows, depth), jnp.bfloat16),
            pltpu.VMEM((slots, strip_size, depth), jnp.bfloat16),
            pltpu.VMEM((CORES * blocks_dev, width, rank_part), jnp.bfloat16),
            pltpu.VMEM((2, nz, slots, width, rank_part), jnp.bfloat16),
            pltpu.VMEM((nz, slots, width, rank_part), jnp.bfloat16),
            pltpu.VMEM((auxes, slots, width, rank_part), jnp.bfloat16),
            pltpu.VMEM((auxes, rows, rank_part), jnp.float32),
            pltpu.VMEM((HALVES, plane - 1, rows, rank_part), jnp.float32),
            pltpu.VMEM((HALVES, rows, rank_part), jnp.float32),
            pltpu.VMEM((2 * pairs - 1, rows, rank_part), jnp.float32),
            dma((5,)),
            dma((2, nz, PIECES)),
            dma((1,)),
            dma((pairs, PIECES)),
            dma((1,)),
            dma((1,)),
            dma((2, nz)),
            dma((2, nz)),
            dma((1,)),
            dma((1,)),
            dma((HALVES,)),
            dma((HALVES,)),
            dma((1,)),
            dma((HALVES,)),
            dma((1,)),
            dma((1,)),
        ],
        compiler_params=pltpu.CompilerParams(
            collective_id=0, has_side_effects=True, vmem_limit_bytes=60 * 2**20
        ),
        name="exchange",
    )(slot_column_block, block_live, integral_strips, x_blocks, aux_factor)

    first_block = (lax.axis_index("pair") * blocks_dev).astype(jnp.int32).reshape(1)
    return pl.pallas_call(
        lambda base, *refs: place_kernel(base, blocks_dev, width // mus, slots, *refs),
        out_shape=jax.ShapeDtypeStruct((rows_x, rank_part), jnp.float32),
        in_specs=[smem, smem, smem, vmem],
        out_specs=vmem,
        name="place",
    )(first_block, slot_row_block, slot_strip_index, sums)


def solution(mesh):
    in_specs = (P("pair", None, "aux"), P(), P(), P(), P(), P("pair", "aux"), P("pair", "aux"))
    out_specs = P("pair", "aux")
    return jax.shard_map(
        per_device, mesh=mesh, in_specs=in_specs, out_specs=out_specs, check_vma=False
    )
```

```python
import functools

import jax
import jax.numpy as jnp
from jax import lax
from jax.experimental import pallas as pl
from jax.experimental.pallas import tpu as pltpu
from jax.sharding import PartitionSpec as P

BLOCK_FUNCTIONS = 128
CORES = 2
HALVES = 2
ROW = 4
PIECES = 4
X_EVERY = PIECES // 2
LEAD = 0
PEER_LAG = 5
SUM_LAG = 4
OTHER_LAG = 4
MESH = pl.DeviceIdType.MESH


def exchange_kernel(
    cols_hbm,
    live_hbm,
    ints_hbm,
    x_hbm,
    z_hbm,
    out_ref,
    cols_ref,
    live_ref,
    zbuf,
    ibuf,
    xchip,
    xin,
    xout,
    xfull,
    prod,
    tpart,
    trecv,
    sbuf,
    fin,
    local_sem,
    z_send,
    z_side,
    z_recv,
    xchip_send,
    xchip_recv,
    xr_send,
    xr_recv,
    xpeer_send,
    xpeer_recv,
    xg_send,
    xg_recv,
    t1_send,
    t1_recv,
    t2_send,
    t2_recv,
):
    pairs = lax.axis_size("pair")
    auxes = lax.axis_size("aux")
    nz = pairs // CORES
    ny = auxes // (HALVES * ROW)
    plane = ny * ROW
    p = lax.axis_index("pair")
    j = lax.axis_index("aux")
    k = p // CORES
    c = p % CORES
    sib = p + 1 - 2 * c
    x = j % ROW
    half = (j // ROW) % HALVES
    y = j // (ROW * HALVES)
    peer = j + (1 - 2 * half) * ROW
    slots = ints_hbm.shape[0]
    blocks_own = x_hbm.shape[0]
    shard_rows = z_hbm.shape[0]
    piece_rows = shard_rows // PIECES
    chunks = shard_rows // BLOCK_FUNCTIONS
    width = BLOCK_FUNCTIONS
    mus = ints_hbm.shape[1] // width
    blocks_chip = CORES * blocks_own

    def aux_of(yy, hh, xx):
        return (yy * HALVES + hh) * ROW + xx

    def plane_aux(rel):
        return aux_of(lax.rem(y + rel // ROW, ny), half, lax.rem(x + rel % ROW, ROW))

    barrier = pltpu.get_barrier_semaphore()

    def greet_line(rel, _):
        pl.semaphore_signal(
            barrier, inc=1, device_id=(lax.rem(p + rel, pairs), j), device_id_type=MESH
        )
        return 0

    lax.fori_loop(1, pairs, greet_line, 0)

    def greet_plane(rel, _):
        pl.semaphore_signal(barrier, inc=1, device_id=(p, plane_aux(rel)), device_id_type=MESH)
        return 0

    lax.fori_loop(1, plane, greet_plane, 0)

    def greet_peers(rel, _):
        pl.semaphore_signal(
            barrier, inc=1, device_id=(lax.rem(p + rel, pairs), peer), device_id_type=MESH
        )
        return 0

    lax.fori_loop(0, pairs, greet_peers, 0)

    load_i = pltpu.make_async_copy(ints_hbm, ibuf, local_sem.at[0])
    load_z = pltpu.make_async_copy(z_hbm, zbuf.at[p], local_sem.at[1])
    own_x = xchip.at[pl.ds(c * blocks_own, blocks_own)]
    load_x = pltpu.make_async_copy(x_hbm, own_x, local_sem.at[2])
    load_cols = pltpu.make_async_copy(cols_hbm, cols_ref, local_sem.at[3])
    load_live = pltpu.make_async_copy(live_hbm, live_ref, local_sem.at[4])
    load_x.start()
    load_cols.start()
    load_live.start()
    load_z.start()
    load_i.start()
    pl.semaphore_wait(barrier, 2 * pairs - 1 + plane - 1)

    def z_copy(direction, shard_chip, piece, own=False):
        rows = pl.ds(pl.multiple_of(piece * piece_rows, piece_rows), piece_rows)
        shard = shard_chip * CORES + c
        src = z_hbm.at[rows] if own else zbuf.at[shard, rows]
        target = p + CORES if direction == 0 else p - CORES
        return pltpu.make_async_remote_copy(
            src_ref=src,
            dst_ref=zbuf.at[shard, rows],
            send_sem=z_send.at[direction, shard_chip, piece],
            recv_sem=z_recv.at[shard, piece],
            device_id=(target, j),
            device_id_type=MESH,
        )

    def z_side_copy(shard_chip, piece, own=False):
        rows = pl.ds(pl.multiple_of(piece * piece_rows, piece_rows), piece_rows)
        shard = shard_chip * CORES + c
        src = z_hbm.at[rows] if own else zbuf.at[shard, rows]
        return pltpu.make_async_remote_copy(
            src_ref=src,
            dst_ref=zbuf.at[shard, rows],
            send_sem=z_side.at[0],
            recv_sem=z_recv.at[shard, piece],
            device_id=(sib, j),
            device_id_type=MESH,
        )

    def z_arrived(shard, piece):
        rows = pl.ds(pl.multiple_of(piece * piece_rows, piece_rows), piece_rows)
        pltpu.make_async_copy(
            zbuf.at[shard, rows], zbuf.at[shard, rows], z_recv.at[shard, piece]
        ).wait()

    x_side = pltpu.make_async_remote_copy(
        src_ref=x_hbm,
        dst_ref=own_x,
        send_sem=xchip_send.at[0],
        recv_sem=xchip_recv.at[0],
        device_id=(sib, j),
        device_id_type=MESH,
    )
    x_side.start()
    for piece in range(PIECES):

        @pl.when(k < nz - 1)
        def _():
            z_copy(0, k, piece, own=True).start()

        @pl.when(k > 0)
        def _():
            z_copy(1, k, piece, own=True).start()

    for piece in range(PIECES):
        z_side_copy(k, piece, own=True).start()

    load_x.wait()
    load_cols.wait()
    load_live.wait()
    pltpu.make_async_copy(own_x, own_x, xchip_recv.at[0]).wait()

    def picked(dest, slot):
        number = (dest * CORES + c) * slots + slot
        local = cols_ref[number] - k * blocks_chip
        near = jnp.minimum(jnp.maximum(local, 0), blocks_chip - 1)
        here = (near == local).astype(jnp.float32)
        return xchip[near].astype(jnp.float32) * here

    def x_copy(direction, dest):
        target = p + CORES if direction == 0 else p - CORES
        return pltpu.make_async_remote_copy(
            src_ref=xout.at[dest],
            dst_ref=xin.at[direction, dest],
            send_sem=xr_send.at[direction, dest],
            recv_sem=xr_recv.at[direction, dest],
            device_id=(target, j),
            device_id_type=MESH,
        )

    def x_arrived(direction, dest):
        pltpu.make_async_copy(
            xin.at[direction, dest], xin.at[direction, dest], xr_recv.at[direction, dest]
        ).wait()

    def x_step(tau, _):
        for direction in range(2):
            place = k if direction == 0 else nz - 1 - k
            far = nz - 1 - tau + place
            dest = far if direction == 0 else nz - 1 - far

            @pl.when(place <= tau)
            def _():
                @pl.when(place > 0)
                def _():
                    x_arrived(direction, dest)
                    for slot in range(slots):
                        got = xin[direction, dest, slot].astype(jnp.float32)
                        xout[dest, slot] = (picked(dest, slot) + got).astype(xout.dtype)

                @pl.when(place == 0)
                def _():
                    for slot in range(slots):
                        xout[dest, slot] = picked(dest, slot).astype(xout.dtype)

                x_copy(direction, dest).start()

        return 0

    lead = min(LEAD, nz - 1)
    lax.fori_loop(0, lead, x_step, 0)

    x_peer = pltpu.make_async_remote_copy(
        src_ref=xout.at[k],
        dst_ref=xfull.at[j],
        send_sem=xpeer_send.at[0],
        recv_sem=xpeer_recv.at[0],
        device_id=(p, peer),
        device_id_type=MESH,
    )

    def x_last():
        for slot in range(slots):
            xout[k, slot] = picked(k, slot).astype(xout.dtype)

        @pl.when(k > 0)
        def _():
            x_arrived(0, k)
            for slot in range(slots):
                total = xout[k, slot].astype(jnp.float32) + xin[0, k, slot].astype(jnp.float32)
                xout[k, slot] = total.astype(xout.dtype)

        @pl.when(k < nz - 1)
        def _():
            x_arrived(1, k)
            for slot in range(slots):
                total = xout[k, slot].astype(jnp.float32) + xin[1, k, slot].astype(jnp.float32)
                xout[k, slot] = total.astype(xout.dtype)

        xfull[j] = xout[k]
        x_peer.start()

    def x_plane(which, which_half):
        def body(rel, _):
            pltpu.make_async_remote_copy(
                src_ref=xfull.at[which],
                dst_ref=xfull.at[which],
                send_sem=xg_send.at[which_half],
                recv_sem=xg_recv.at[which_half],
                device_id=(p, plane_aux(rel)),
                device_id_type=MESH,
            ).start()
            return 0

        lax.fori_loop(1, plane, body, 0)

    def x_plane_arrived(which_half):
        some = xfull.at[pl.ds(0, plane - 1)]
        pltpu.make_async_copy(some, some, xg_recv.at[which_half]).wait()

    def multiply(shard):
        z = zbuf[shard]
        for slot in range(slots):
            prod[shard, slot] = lax.dot_general(
                ibuf[slot], z, (((1,), (1,)), ((), ())), preferred_element_type=jnp.float32
            )

    def contract(shard):
        for slot in range(slots):
            alive = live_ref[p * slots + slot].astype(jnp.float32)
            for h in range(chunks):
                chunk = shard * chunks + h
                rows = xfull[chunk, slot].astype(jnp.float32)
                part = prod[shard, slot, :, h * width : (h + 1) * width]
                part = part.reshape(mus, width, width)
                term = jnp.sum(part * rows[None], axis=1) * alive
                tpart[chunk, slot * mus : (slot + 1) * mus, :] = term
        for h in range(chunks):
            chunk = shard * chunks + h
            yy = chunk // (HALVES * ROW)
            hh = (chunk // ROW) % HALVES
            xx = chunk % ROW
            rel = lax.rem(y - yy + ny, ny) * ROW + lax.rem(x - xx + ROW, ROW)

            @pl.when(rel > 0)
            def _():
                pltpu.make_async_remote_copy(
                    src_ref=tpart.at[chunk],
                    dst_ref=trecv.at[hh, rel - 1],
                    send_sem=t1_send.at[0],
                    recv_sem=t1_recv.at[hh],
                    device_id=(p, aux_of(yy, half, xx)),
                    device_id_type=MESH,
                ).start()

    def for_set(step, first, last, what):
        def one(n, _):
            direction = n // CORES
            core = lax.rem(c + n, CORES)
            chip = jnp.where(direction == 0, k - step, k + step)
            shard = chip * CORES + core
            valid = jnp.logical_and(chip >= 0, chip < nz)
            valid = jnp.logical_and(valid, jnp.logical_or(step > 0, direction == 0))

            @pl.when(valid)
            def _():
                what(shard, core)

            return 0

        lax.fori_loop(first, last, one, 0)

    def multiply_arrived(shard, core):
        @pl.when(core != c)
        def _():
            for piece in range(PIECES):
                z_arrived(shard, piece)

        multiply(shard)

    def contract_ready(shard, core):
        contract(shard)

    load_z.wait()
    load_i.wait()

    early = nz // 2 - 1
    ready = PIECES * (nz - 2) + 1
    done_at = [ready] * early + [min(ready + OTHER_LAG, PIECES * (nz - 1) - 1)] * early
    done_at += [PIECES * (nz - 1) - 1, PIECES * (nz - 1)]
    own_parity = lax.rem(half + k, 2)

    def step_of(item):
        own = own_parity + 2 * item
        other = 1 - own_parity + 2 * (item - early)
        return jnp.where(item < early, own, jnp.where(item < 2 * early, other, item))

    def item_of(step):
        own = lax.rem(step + own_parity, 2) == 0
        listed = jnp.where(own, (step - own_parity) // 2, early + (step - 1 + own_parity) // 2)
        return jnp.where(step < 2 * early, listed, step)

    def finished_at(item):
        event = jnp.int32(done_at[0])
        for n in range(1, nz):
            event = jnp.where(item >= n, done_at[n], event)
        return event

    def items_by(event):
        count = jnp.int32(0)
        for n in range(nz):
            count = count + (event >= done_at[n]).astype(jnp.int32)
        return count

    last_event = PIECES * (nz - 1) + 1
    x_event = X_EVERY * (nz - 1 - lead)
    shares = 2 * CORES // PIECES
    peer_event = min(x_event + PEER_LAG, done_at[early])

    def spread(hh):
        pltpu.make_async_copy(trecv.at[hh], trecv.at[hh], t1_recv.at[hh]).wait()
        sbuf[hh] = jnp.sum(trecv[hh], axis=0) + tpart[aux_of(y, hh, x)]
        near = jnp.where(half == hh, 1, 0)

        def send(rel, _):
            slot = jnp.where(half == hh, pairs - 1 - rel, pairs - 1 + lax.rem(pairs - rel, pairs))
            pltpu.make_async_remote_copy(
                src_ref=sbuf.at[hh],
                dst_ref=fin.at[slot],
                send_sem=t2_send.at[0],
                recv_sem=t2_recv.at[0],
                device_id=(lax.rem(p + rel, pairs), aux_of(y, hh, x)),
                device_id_type=MESH,
            ).start()
            return 0

        lax.fori_loop(near, pairs, send, 0)

    def event_step(event, _):
        t = event // PIECES + 1
        piece = lax.rem(event, PIECES)

        @pl.when(k - t >= 0)
        def _():
            z_arrived((k - t) * CORES + c, piece)

            @pl.when(k < nz - 1)
            def _():
                z_copy(0, k - t, piece).start()

            z_side_copy(k - t, piece).start()

        @pl.when(k + t < nz)
        def _():
            z_arrived((k + t) * CORES + c, piece)

            @pl.when(k > 0)
            def _():
                z_copy(1, k + t, piece).start()

            z_side_copy(k + t, piece).start()

        @pl.when(jnp.logical_and(event < x_event, lax.rem(event, X_EVERY) == 0))
        def _():
            x_step(event // X_EVERY + lead, 0)

        @pl.when(event == x_event)
        def _():
            x_last()
            x_plane(j, 0)

        @pl.when(event == peer_event)
        def _():
            pltpu.make_async_copy(xfull.at[0], xfull.at[0], xpeer_recv.at[0]).wait()
            x_plane(peer, 1)

        @pl.when(event == done_at[0])
        def _():
            x_plane_arrived(0)

        @pl.when(event == done_at[early])
        def _():
            x_plane_arrived(1)

        for hh in range(HALVES):
            step = jnp.abs(k - aux_of(y, hh, x) // (chunks * CORES))

            @pl.when(event == jnp.minimum(finished_at(item_of(step)) + SUM_LAG, last_event))
            def _():
                spread(hh)

        ending = event == PIECES * (nz - 1)
        first = jnp.where(ending, 0, piece * shares)
        last = jnp.where(ending, 2 * CORES, (piece + 1) * shares)
        for_set(t - 1, first, jnp.where(event > PIECES * (nz - 1), 0, last), multiply_arrived)

        def work(item, _):
            for_set(step_of(item), 0, 2 * CORES, contract_ready)
            return 0

        lax.fori_loop(items_by(event - 1), items_by(event), work, 0)

        return 0

    lax.fori_loop(0, last_event + 1, event_step, 0)

    pltpu.make_async_copy(fin, fin, t2_recv.at[0]).wait()
    out_ref[p] = sbuf[half] + fin[pairs - 1]

    def take(rel, _):
        out_ref[lax.rem(p + rel, pairs)] = fin[rel - 1] + fin[pairs - 1 + rel]
        return 0

    lax.fori_loop(1, pairs, take, 0)

    x_side.wait_send()
    x_peer.wait_send()
    pltpu.make_async_copy(fin, fin, t2_send.at[0]).wait()
    pltpu.make_async_copy(trecv, trecv, t1_send.at[0]).wait()
    sent = xfull.at[pl.ds(0, plane - 1)]
    for which in range(HALVES):
        pltpu.make_async_copy(sent, sent, xg_send.at[which]).wait()
    sent_z = zbuf.at[pl.ds(0, nz)]
    pltpu.make_async_copy(sent_z, sent_z, z_side.at[0]).wait()

    def z_sent(chip, _):
        @pl.when(jnp.logical_and(chip <= k, k < nz - 1))
        def _():
            for piece in range(PIECES):
                z_copy(0, chip, piece).wait_send()

        @pl.when(jnp.logical_and(chip >= k, k > 0))
        def _():
            for piece in range(PIECES):
                z_copy(1, chip, piece).wait_send()

        @pl.when(chip > k)
        def _():
            x_copy(0, chip).wait_send()

        @pl.when(chip < k)
        def _():
            x_copy(1, chip).wait_send()

        return 0

    lax.fori_loop(0, nz, z_sent, 0)


def place_kernel(first_block, blocks_dev, strips, slots, rows_ref, strip_ref, sums_ref, out_ref):
    out_ref[...] = jnp.zeros_like(out_ref)
    base = first_block[0]
    rows, columns = sums_ref.shape[1:]
    mus = rows // slots
    sublane = lax.broadcasted_iota(jnp.int32, (rows, columns), 0) // mus

    def body(p, _):
        value = sums_ref[p]
        turned = pltpu.roll(value, mus, 0)
        for slot in range(slots):
            number = p * slots + slot
            local = rows_ref[number] - base
            strip = local * strips + strip_ref[number]
            part = strip % slots
            tile = strip // slots

            @pl.when(jnp.logical_and(local >= 0, local < blocks_dev))
            def _():
                moved = jnp.where(part == slot, value, turned)
                kept = jnp.where(sublane == part, moved, 0.0)
                at = pl.ds(pl.multiple_of(tile * rows, rows), rows)
                out_ref[at, :] = out_ref[at, :] + kept

        return 0

    lax.fori_loop(0, sums_ref.shape[0], body, 0)


def per_device(
    integral_strips,
    slot_row_block,
    slot_strip_index,
    slot_column_block,
    block_live,
    ao_factor,
    aux_factor,
):
    slots, strip_size, depth = integral_strips.shape
    width = BLOCK_FUNCTIONS
    mus = strip_size // width
    pairs = lax.axis_size("pair")
    auxes = lax.axis_size("aux")
    nz = pairs // CORES
    plane = auxes // HALVES
    shard_rows = aux_factor.shape[0]
    rows_x, rank_part = ao_factor.shape
    blocks_dev = rows_x // width
    x_blocks = ao_factor.reshape(blocks_dev, width, rank_part)
    smem = pl.BlockSpec(memory_space=pltpu.SMEM)
    hbm = pl.BlockSpec(memory_space=pltpu.HBM)
    vmem = pl.BlockSpec(memory_space=pltpu.VMEM)
    rows = slots * mus
    dma = pltpu.SemaphoreType.DMA
    sums = pl.pallas_call(
        exchange_kernel,
        out_shape=jax.ShapeDtypeStruct((pairs, rows, rank_part), jnp.float32),
        in_specs=[hbm, hbm, hbm, hbm, hbm],
        out_specs=vmem,
        scratch_shapes=[
            pltpu.SMEM((slot_column_block.shape[0],), jnp.int32),
            pltpu.SMEM((block_live.shape[0],), jnp.int32),
            pltpu.VMEM((pairs, shard_rows, depth), jnp.bfloat16),
            pltpu.VMEM((slots, strip_size, depth), jnp.bfloat16),
            pltpu.VMEM((CORES * blocks_dev, width, rank_part), jnp.bfloat16),
            pltpu.VMEM((2, nz, slots, width, rank_part), jnp.bfloat16),
            pltpu.VMEM((nz, slots, width, rank_part), jnp.bfloat16),
            pltpu.VMEM((auxes, slots, width, rank_part), jnp.bfloat16),
            pltpu.VMEM((pairs, slots, strip_size, shard_rows), jnp.float32),
            pltpu.VMEM((auxes, rows, rank_part), jnp.float32),
            pltpu.VMEM((HALVES, plane - 1, rows, rank_part), jnp.float32),
            pltpu.VMEM((HALVES, rows, rank_part), jnp.float32),
            pltpu.VMEM((2 * pairs - 1, rows, rank_part), jnp.float32),
            dma((5,)),
            dma((2, nz, PIECES)),
            dma((1,)),
            dma((pairs, PIECES)),
            dma((1,)),
            dma((1,)),
            dma((2, nz)),
            dma((2, nz)),
            dma((1,)),
            dma((1,)),
            dma((HALVES,)),
            dma((HALVES,)),
            dma((1,)),
            dma((HALVES,)),
            dma((1,)),
            dma((1,)),
        ],
        compiler_params=pltpu.CompilerParams(
            collective_id=0, has_side_effects=True, vmem_limit_bytes=60 * 2**20
        ),
        name="exchange",
    )(slot_column_block, block_live, integral_strips, x_blocks, aux_factor)

    first_block = (lax.axis_index("pair") * blocks_dev).astype(jnp.int32).reshape(1)
    return pl.pallas_call(
        lambda base, *refs: place_kernel(base, blocks_dev, width // mus, slots, *refs),
        out_shape=jax.ShapeDtypeStruct((rows_x, rank_part), jnp.float32),
        in_specs=[smem, smem, smem, vmem],
        out_specs=vmem,
        name="place",
    )(first_block, slot_row_block, slot_strip_index, sums)


def solution(mesh):
    in_specs = (P("pair", None, "aux"), P(), P(), P(), P(), P("pair", "aux"), P("pair", "aux"))
    out_specs = P("pair", "aux")
    return jax.shard_map(
        per_device, mesh=mesh, in_specs=in_specs, out_specs=out_specs, check_vma=False
    )
```

```python
import functools

import jax
import jax.numpy as jnp
from jax import lax
from jax.experimental import pallas as pl
from jax.experimental.pallas import tpu as pltpu
from jax.sharding import PartitionSpec as P

BLOCK_FUNCTIONS = 128
CORES = 2
HALVES = 2
ROW = 4
PIECES = 4
X_EVERY = PIECES // 2
LEAD = 0
PEER_LAG = 5
WORD_EVENTS = (0, 2, 5, 9)
SUM_LAG = 4
MESH = pl.DeviceIdType.MESH


def exchange_kernel(
    cols_hbm,
    live_hbm,
    ints_hbm,
    x_hbm,
    z_hbm,
    out_ref,
    cols_ref,
    live_ref,
    zbuf,
    ibuf,
    xchip,
    xin,
    xout,
    xfull,
    prod,
    tpart,
    trecv,
    sbuf,
    fin,
    local_sem,
    z_send,
    z_side,
    z_recv,
    xchip_send,
    xchip_recv,
    xr_send,
    xr_recv,
    xpeer_send,
    xpeer_recv,
    xg_send,
    xg_recv,
    t1_send,
    t1_recv,
    t2_send,
    t2_recv,
    word_sem,
):
    pairs = lax.axis_size("pair")
    auxes = lax.axis_size("aux")
    nz = pairs // CORES
    ny = auxes // (HALVES * ROW)
    plane = ny * ROW
    p = lax.axis_index("pair")
    j = lax.axis_index("aux")
    k = p // CORES
    c = p % CORES
    sib = p + 1 - 2 * c
    x = j % ROW
    half = (j // ROW) % HALVES
    y = j // (ROW * HALVES)
    peer = j + (1 - 2 * half) * ROW
    slots = ints_hbm.shape[0]
    blocks_own = x_hbm.shape[0]
    shard_rows = z_hbm.shape[0]
    piece_rows = shard_rows // PIECES
    chunks = shard_rows // BLOCK_FUNCTIONS
    width = BLOCK_FUNCTIONS
    mus = ints_hbm.shape[1] // width
    blocks_chip = CORES * blocks_own

    def aux_of(yy, hh, xx):
        return (yy * HALVES + hh) * ROW + xx

    def plane_aux(rel):
        return aux_of(lax.rem(y + rel // ROW, ny), half, lax.rem(x + rel % ROW, ROW))

    barrier = pltpu.get_barrier_semaphore()

    def ring(hops):
        z = lax.rem(half * nz + k + hops + HALVES * nz, HALVES * nz)
        return lax.rem(z, nz) * CORES + c, aux_of(y, z // nz, x)

    def across(hops):
        return p, aux_of(y, half, lax.rem(x + hops + ROW, ROW))

    def along(hops):
        return p, aux_of(lax.rem(y + hops + ny, ny), half, x)

    def greet(semaphore, devices):
        for device in devices:
            pl.semaphore_signal(semaphore, inc=1, device_id=device, device_id_type=MESH)

    greet(barrier, [ring(1), ring(-1), (sib, j), across(1), across(-1), along(1), along(-1)])

    word = [
        [(word_sem.at[0], [across(1), across(-1)]), (word_sem.at[1], [ring(1), ring(-1)])],
        [(word_sem.at[2], [along(1), along(-1)]), (word_sem.at[3], [ring(2), ring(-2)])],
        [(word_sem.at[4], [along(1), along(-1)]), (word_sem.at[5], [ring(4), ring(-4)])],
    ]

    def pass_word(turn):
        if turn > 0:
            for semaphore, devices in word[turn - 1]:
                pl.semaphore_wait(semaphore, len(devices))
        if turn < len(word):
            for semaphore, devices in word[turn]:
                greet(semaphore, devices)

    load_i = pltpu.make_async_copy(ints_hbm, ibuf, local_sem.at[0])
    load_z = pltpu.make_async_copy(z_hbm, zbuf.at[p], local_sem.at[1])
    own_x = xchip.at[pl.ds(c * blocks_own, blocks_own)]
    load_x = pltpu.make_async_copy(x_hbm, own_x, local_sem.at[2])
    load_cols = pltpu.make_async_copy(cols_hbm, cols_ref, local_sem.at[3])
    load_live = pltpu.make_async_copy(live_hbm, live_ref, local_sem.at[4])
    load_x.start()
    load_cols.start()
    load_live.start()
    load_z.start()
    load_i.start()
    pl.semaphore_wait(barrier, 7)

    def z_copy(direction, shard_chip, piece, own=False):
        rows = pl.ds(pl.multiple_of(piece * piece_rows, piece_rows), piece_rows)
        shard = shard_chip * CORES + c
        src = z_hbm.at[rows] if own else zbuf.at[shard, rows]
        target = p + CORES if direction == 0 else p - CORES
        return pltpu.make_async_remote_copy(
            src_ref=src,
            dst_ref=zbuf.at[shard, rows],
            send_sem=z_send.at[direction, shard_chip, piece],
            recv_sem=z_recv.at[shard, piece],
            device_id=(target, j),
            device_id_type=MESH,
        )

    def z_side_copy(shard_chip, piece, own=False):
        rows = pl.ds(pl.multiple_of(piece * piece_rows, piece_rows), piece_rows)
        shard = shard_chip * CORES + c
        src = z_hbm.at[rows] if own else zbuf.at[shard, rows]
        return pltpu.make_async_remote_copy(
            src_ref=src,
            dst_ref=zbuf.at[shard, rows],
            send_sem=z_side.at[0],
            recv_sem=z_recv.at[shard, piece],
            device_id=(sib, j),
            device_id_type=MESH,
        )

    def z_arrived(shard, piece):
        rows = pl.ds(pl.multiple_of(piece * piece_rows, piece_rows), piece_rows)
        pltpu.make_async_copy(
            zbuf.at[shard, rows], zbuf.at[shard, rows], z_recv.at[shard, piece]
        ).wait()

    x_side = pltpu.make_async_remote_copy(
        src_ref=x_hbm,
        dst_ref=own_x,
        send_sem=xchip_send.at[0],
        recv_sem=xchip_recv.at[0],
        device_id=(sib, j),
        device_id_type=MESH,
    )
    x_side.start()
    for piece in range(PIECES):

        @pl.when(k < nz - 1)
        def _():
            z_copy(0, k, piece, own=True).start()

        @pl.when(k > 0)
        def _():
            z_copy(1, k, piece, own=True).start()

    for piece in range(PIECES):
        z_side_copy(k, piece, own=True).start()

    load_x.wait()
    load_cols.wait()
    load_live.wait()
    pltpu.make_async_copy(own_x, own_x, xchip_recv.at[0]).wait()

    def picked(dest, slot):
        number = (dest * CORES + c) * slots + slot
        local = cols_ref[number] - k * blocks_chip
        near = jnp.minimum(jnp.maximum(local, 0), blocks_chip - 1)
        here = (near == local).astype(jnp.float32)
        return xchip[near].astype(jnp.float32) * here

    def x_copy(direction, dest):
        target = p + CORES if direction == 0 else p - CORES
        return pltpu.make_async_remote_copy(
            src_ref=xout.at[dest],
            dst_ref=xin.at[direction, dest],
            send_sem=xr_send.at[direction, dest],
            recv_sem=xr_recv.at[direction, dest],
            device_id=(target, j),
            device_id_type=MESH,
        )

    def x_arrived(direction, dest):
        pltpu.make_async_copy(
            xin.at[direction, dest], xin.at[direction, dest], xr_recv.at[direction, dest]
        ).wait()

    def x_step(tau, _):
        for direction in range(2):
            place = k if direction == 0 else nz - 1 - k
            far = nz - 1 - tau + place
            dest = far if direction == 0 else nz - 1 - far

            @pl.when(place <= tau)
            def _():
                @pl.when(place > 0)
                def _():
                    x_arrived(direction, dest)
                    for slot in range(slots):
                        got = xin[direction, dest, slot].astype(jnp.float32)
                        xout[dest, slot] = (picked(dest, slot) + got).astype(xout.dtype)

                @pl.when(place == 0)
                def _():
                    for slot in range(slots):
                        xout[dest, slot] = picked(dest, slot).astype(xout.dtype)

                x_copy(direction, dest).start()

        return 0

    lead = min(LEAD, nz - 1)
    lax.fori_loop(0, lead, x_step, 0)

    x_peer = pltpu.make_async_remote_copy(
        src_ref=xout.at[k],
        dst_ref=xfull.at[j],
        send_sem=xpeer_send.at[0],
        recv_sem=xpeer_recv.at[0],
        device_id=(p, peer),
        device_id_type=MESH,
    )

    def x_last():
        for slot in range(slots):
            xout[k, slot] = picked(k, slot).astype(xout.dtype)

        @pl.when(k > 0)
        def _():
            x_arrived(0, k)
            for slot in range(slots):
                total = xout[k, slot].astype(jnp.float32) + xin[0, k, slot].astype(jnp.float32)
                xout[k, slot] = total.astype(xout.dtype)

        @pl.when(k < nz - 1)
        def _():
            x_arrived(1, k)
            for slot in range(slots):
                total = xout[k, slot].astype(jnp.float32) + xin[1, k, slot].astype(jnp.float32)
                xout[k, slot] = total.astype(xout.dtype)

        xfull[j] = xout[k]
        x_peer.start()

    def x_plane(which, which_half):
        def body(rel, _):
            pltpu.make_async_remote_copy(
                src_ref=xfull.at[which],
                dst_ref=xfull.at[which],
                send_sem=xg_send.at[which_half],
                recv_sem=xg_recv.at[which_half],
                device_id=(p, plane_aux(rel)),
                device_id_type=MESH,
            ).start()
            return 0

        lax.fori_loop(1, plane, body, 0)

    def x_plane_arrived(which_half):
        some = xfull.at[pl.ds(0, plane - 1)]
        pltpu.make_async_copy(some, some, xg_recv.at[which_half]).wait()

    def multiply(shard):
        z = zbuf[shard]
        for slot in range(slots):
            prod[shard, slot] = lax.dot_general(
                ibuf[slot], z, (((1,), (1,)), ((), ())), preferred_element_type=jnp.float32
            )

    def contract(shard):
        for slot in range(slots):
            alive = live_ref[p * slots + slot].astype(jnp.float32)
            for h in range(chunks):
                chunk = shard * chunks + h
                rows = xfull[chunk, slot].astype(jnp.float32)
                part = prod[shard, slot, :, h * width : (h + 1) * width]
                part = part.reshape(mus, width, width)
                term = jnp.sum(part * rows[None], axis=1) * alive
                tpart[chunk, slot * mus : (slot + 1) * mus, :] = term
        for h in range(chunks):
            chunk = shard * chunks + h
            yy = chunk // (HALVES * ROW)
            hh = (chunk // ROW) % HALVES
            xx = chunk % ROW
            rel = lax.rem(y - yy + ny, ny) * ROW + lax.rem(x - xx + ROW, ROW)

            @pl.when(rel > 0)
            def _():
                pltpu.make_async_remote_copy(
                    src_ref=tpart.at[chunk],
                    dst_ref=trecv.at[hh, rel - 1],
                    send_sem=t1_send.at[0],
                    recv_sem=t1_recv.at[hh],
                    device_id=(p, aux_of(yy, half, xx)),
                    device_id_type=MESH,
                ).start()

    def for_set(step, first, last, what):
        def one(n, _):
            direction = n // CORES
            core = lax.rem(c + n, CORES)
            chip = jnp.where((direction == 0) == (k >= nz // 2), k - step, k + step)
            shard = chip * CORES + core
            valid = jnp.logical_and(chip >= 0, chip < nz)
            valid = jnp.logical_and(valid, jnp.logical_or(step > 0, direction == 0))

            @pl.when(valid)
            def _():
                what(shard, core)

            return 0

        lax.fori_loop(first, last, one, 0)

    def multiply_arrived(shard, core):
        @pl.when(core != c)
        def _():
            for piece in range(PIECES):
                z_arrived(shard, piece)

        multiply(shard)

    def contract_ready(shard, core):
        contract(shard)

    load_z.wait()
    load_i.wait()

    early = nz // 2 - 1
    ready = PIECES * (nz - 2)
    done_at = [ready] * early + [ready + 2] * (early + 1) + [PIECES * (nz - 1)]
    own_parity = lax.rem(half + k, 2)

    def step_of(item):
        own = own_parity + 2 * item
        other = 1 - own_parity + 2 * (item - early)
        return jnp.where(item < early, own, jnp.where(item < 2 * early, other, item))

    def item_of(step):
        own = lax.rem(step + own_parity, 2) == 0
        listed = jnp.where(own, (step - own_parity) // 2, early + (step - 1 + own_parity) // 2)
        return jnp.where(step < 2 * early, listed, step)

    def finished_at(item):
        event = jnp.int32(done_at[0])
        for n in range(1, nz):
            event = jnp.where(item >= n, done_at[n], event)
        return event

    def items_by(event):
        count = jnp.int32(0)
        for n in range(nz):
            count = count + (event >= done_at[n]).astype(jnp.int32)
        return count

    last_event = PIECES * (nz - 1) + 1
    x_event = X_EVERY * (nz - 1 - lead)
    shares = 2 * CORES // PIECES
    peer_event = min(x_event + PEER_LAG, done_at[early])

    def spread(hh):
        pltpu.make_async_copy(trecv.at[hh], trecv.at[hh], t1_recv.at[hh]).wait()
        sbuf[hh] = jnp.sum(trecv[hh], axis=0) + tpart[aux_of(y, hh, x)]
        near = jnp.where(half == hh, 1, 0)

        def send(rel, _):
            slot = jnp.where(half == hh, pairs - 1 - rel, pairs - 1 + lax.rem(pairs - rel, pairs))
            pltpu.make_async_remote_copy(
                src_ref=sbuf.at[hh],
                dst_ref=fin.at[slot],
                send_sem=t2_send.at[0],
                recv_sem=t2_recv.at[0],
                device_id=(lax.rem(p + rel, pairs), aux_of(y, hh, x)),
                device_id_type=MESH,
            ).start()
            return 0

        lax.fori_loop(near, pairs, send, 0)

    def event_step(event, _):
        t = event // PIECES + 1
        piece = lax.rem(event, PIECES)

        @pl.when(k - t >= 0)
        def _():
            z_arrived((k - t) * CORES + c, piece)

            @pl.when(k < nz - 1)
            def _():
                z_copy(0, k - t, piece).start()

            z_side_copy(k - t, piece).start()

        @pl.when(k + t < nz)
        def _():
            z_arrived((k + t) * CORES + c, piece)

            @pl.when(k > 0)
            def _():
                z_copy(1, k + t, piece).start()

            z_side_copy(k + t, piece).start()

        @pl.when(jnp.logical_and(event < x_event, lax.rem(event, X_EVERY) == 0))
        def _():
            x_step(event // X_EVERY + lead, 0)

        for turn, at in enumerate(WORD_EVENTS):

            @pl.when(event == min(at, x_event))
            def _():
                pass_word(turn)

        @pl.when(event == x_event)
        def _():
            x_last()
            x_plane(j, 0)

        @pl.when(event == peer_event)
        def _():
            pltpu.make_async_copy(xfull.at[0], xfull.at[0], xpeer_recv.at[0]).wait()
            x_plane(peer, 1)

        @pl.when(event == done_at[0])
        def _():
            x_plane_arrived(0)

        @pl.when(event == done_at[early])
        def _():
            x_plane_arrived(1)

        for hh in range(HALVES):
            step = jnp.abs(k - aux_of(y, hh, x) // (chunks * CORES))

            @pl.when(event == jnp.minimum(finished_at(item_of(step)) + SUM_LAG, last_event))
            def _():
                spread(hh)

        ending = event == PIECES * (nz - 1)
        first = jnp.where(ending, 0, piece * shares)
        last = jnp.where(ending, 2 * CORES, (piece + 1) * shares)
        for_set(t - 1, first, jnp.where(event > PIECES * (nz - 1), 0, last), multiply_arrived)

        def work(item, _):
            for_set(step_of(item), 0, 2 * CORES, contract_ready)
            return 0

        lax.fori_loop(items_by(event - 1), items_by(event), work, 0)

        return 0

    lax.fori_loop(0, last_event + 1, event_step, 0)

    pltpu.make_async_copy(fin, fin, t2_recv.at[0]).wait()
    out_ref[p] = sbuf[half] + fin[pairs - 1]

    def take(rel, _):
        out_ref[lax.rem(p + rel, pairs)] = fin[rel - 1] + fin[pairs - 1 + rel]
        return 0

    lax.fori_loop(1, pairs, take, 0)

    x_side.wait_send()
    x_peer.wait_send()
    pltpu.make_async_copy(fin, fin, t2_send.at[0]).wait()
    pltpu.make_async_copy(trecv, trecv, t1_send.at[0]).wait()
    sent = xfull.at[pl.ds(0, plane - 1)]
    for which in range(HALVES):
        pltpu.make_async_copy(sent, sent, xg_send.at[which]).wait()
    sent_z = zbuf.at[pl.ds(0, nz)]
    pltpu.make_async_copy(sent_z, sent_z, z_side.at[0]).wait()

    def z_sent(chip, _):
        @pl.when(jnp.logical_and(chip <= k, k < nz - 1))
        def _():
            for piece in range(PIECES):
                z_copy(0, chip, piece).wait_send()

        @pl.when(jnp.logical_and(chip >= k, k > 0))
        def _():
            for piece in range(PIECES):
                z_copy(1, chip, piece).wait_send()

        @pl.when(chip > k)
        def _():
            x_copy(0, chip).wait_send()

        @pl.when(chip < k)
        def _():
            x_copy(1, chip).wait_send()

        return 0

    lax.fori_loop(0, nz, z_sent, 0)


def place_kernel(first_block, blocks_dev, strips, slots, rows_ref, strip_ref, sums_ref, out_ref):
    out_ref[...] = jnp.zeros_like(out_ref)
    base = first_block[0]
    rows, columns = sums_ref.shape[1:]
    mus = rows // slots
    sublane = lax.broadcasted_iota(jnp.int32, (rows, columns), 0) // mus

    def body(p, _):
        value = sums_ref[p]
        turned = pltpu.roll(value, mus, 0)
        for slot in range(slots):
            number = p * slots + slot
            local = rows_ref[number] - base
            strip = local * strips + strip_ref[number]
            part = strip % slots
            tile = strip // slots

            @pl.when(jnp.logical_and(local >= 0, local < blocks_dev))
            def _():
                moved = jnp.where(part == slot, value, turned)
                kept = jnp.where(sublane == part, moved, 0.0)
                at = pl.ds(pl.multiple_of(tile * rows, rows), rows)
                out_ref[at, :] = out_ref[at, :] + kept

        return 0

    lax.fori_loop(0, sums_ref.shape[0], body, 0)


def per_device(
    integral_strips,
    slot_row_block,
    slot_strip_index,
    slot_column_block,
    block_live,
    ao_factor,
    aux_factor,
):
    slots, strip_size, depth = integral_strips.shape
    width = BLOCK_FUNCTIONS
    mus = strip_size // width
    pairs = lax.axis_size("pair")
    auxes = lax.axis_size("aux")
    nz = pairs // CORES
    plane = auxes // HALVES
    shard_rows = aux_factor.shape[0]
    rows_x, rank_part = ao_factor.shape
    blocks_dev = rows_x // width
    x_blocks = ao_factor.reshape(blocks_dev, width, rank_part)
    smem = pl.BlockSpec(memory_space=pltpu.SMEM)
    hbm = pl.BlockSpec(memory_space=pltpu.HBM)
    vmem = pl.BlockSpec(memory_space=pltpu.VMEM)
    rows = slots * mus
    dma = pltpu.SemaphoreType.DMA
    sums = pl.pallas_call(
        exchange_kernel,
        out_shape=jax.ShapeDtypeStruct((pairs, rows, rank_part), jnp.float32),
        in_specs=[hbm, hbm, hbm, hbm, hbm],
        out_specs=vmem,
        scratch_shapes=[
            pltpu.SMEM((slot_column_block.shape[0],), jnp.int32),
            pltpu.SMEM((block_live.shape[0],), jnp.int32),
            pltpu.VMEM((pairs, shard_rows, depth), jnp.bfloat16),
            pltpu.VMEM((slots, strip_size, depth), jnp.bfloat16),
            pltpu.VMEM((CORES * blocks_dev, width, rank_part), jnp.bfloat16),
            pltpu.VMEM((2, nz, slots, width, rank_part), jnp.bfloat16),
            pltpu.VMEM((nz, slots, width, rank_part), jnp.bfloat16),
            pltpu.VMEM((auxes, slots, width, rank_part), jnp.bfloat16),
            pltpu.VMEM((pairs, slots, strip_size, shard_rows), jnp.float32),
            pltpu.VMEM((auxes, rows, rank_part), jnp.float32),
            pltpu.VMEM((HALVES, plane - 1, rows, rank_part), jnp.float32),
            pltpu.VMEM((HALVES, rows, rank_part), jnp.float32),
            pltpu.VMEM((2 * pairs - 1, rows, rank_part), jnp.float32),
            dma((5,)),
            dma((2, nz, PIECES)),
            dma((1,)),
            dma((pairs, PIECES)),
            dma((1,)),
            dma((1,)),
            dma((2, nz)),
            dma((2, nz)),
            dma((1,)),
            dma((1,)),
            dma((HALVES,)),
            dma((HALVES,)),
            dma((1,)),
            dma((HALVES,)),
            dma((1,)),
            dma((1,)),
            pltpu.SemaphoreType.REGULAR((6,)),
        ],
        compiler_params=pltpu.CompilerParams(
            collective_id=0, has_side_effects=True, vmem_limit_bytes=60 * 2**20
        ),
        name="exchange",
    )(slot_column_block, block_live, integral_strips, x_blocks, aux_factor)

    first_block = (lax.axis_index("pair") * blocks_dev).astype(jnp.int32).reshape(1)
    return pl.pallas_call(
        lambda base, *refs: place_kernel(base, blocks_dev, width // mus, slots, *refs),
        out_shape=jax.ShapeDtypeStruct((rows_x, rank_part), jnp.float32),
        in_specs=[smem, smem, smem, vmem],
        out_specs=vmem,
        name="place",
    )(first_block, slot_row_block, slot_strip_index, sums)


def solution(mesh):
    in_specs = (P("pair", None, "aux"), P(), P(), P(), P(), P("pair", "aux"), P("pair", "aux"))
    out_specs = P("pair", "aux")
    return jax.shard_map(
        per_device, mesh=mesh, in_specs=in_specs, out_specs=out_specs, check_vma=False
    )
```

```python
import functools

import jax
import jax.numpy as jnp
from jax import lax
from jax.experimental import pallas as pl
from jax.experimental.pallas import tpu as pltpu
from jax.sharding import PartitionSpec as P

BLOCK_FUNCTIONS = 128
CORES = 2
HALVES = 2
ROW = 4
PIECES = 4
X_EVERY = PIECES // 2
LEAD = 0
PEER_LAG = 5
ON_LAG = 3
WORD_EVENTS = (0, 2, 5, 9)
SUM_LAG = 4
MESH = pl.DeviceIdType.MESH


def exchange_kernel(
    cols_hbm,
    live_hbm,
    ints_hbm,
    x_hbm,
    z_hbm,
    out_ref,
    cols_ref,
    live_ref,
    zbuf,
    ibuf,
    xchip,
    xin,
    xout,
    xfull,
    prod,
    tpart,
    trecv,
    sbuf,
    fin,
    local_sem,
    z_send,
    z_side,
    z_recv,
    xchip_send,
    xchip_recv,
    xr_send,
    xr_recv,
    xpeer_send,
    xpeer_recv,
    xg_send,
    xg_recv,
    t1_send,
    t1_recv,
    t2_send,
    t2_recv,
    word_sem,
):
    pairs = lax.axis_size("pair")
    auxes = lax.axis_size("aux")
    nz = pairs // CORES
    ny = auxes // (HALVES * ROW)
    plane = ny * ROW
    p = lax.axis_index("pair")
    j = lax.axis_index("aux")
    k = p // CORES
    c = p % CORES
    sib = p + 1 - 2 * c
    x = j % ROW
    half = (j // ROW) % HALVES
    y = j // (ROW * HALVES)
    peer = j + (1 - 2 * half) * ROW
    slots = ints_hbm.shape[0]
    blocks_own = x_hbm.shape[0]
    shard_rows = z_hbm.shape[0]
    piece_rows = shard_rows // PIECES
    chunks = shard_rows // BLOCK_FUNCTIONS
    width = BLOCK_FUNCTIONS
    mus = ints_hbm.shape[1] // width
    blocks_chip = CORES * blocks_own

    def aux_of(yy, hh, xx):
        return (yy * HALVES + hh) * ROW + xx

    def plane_aux(rel):
        return aux_of(lax.rem(y + rel // ROW, ny), half, lax.rem(x + rel % ROW, ROW))

    barrier = pltpu.get_barrier_semaphore()

    def ring(hops):
        z = lax.rem(half * nz + k + hops + HALVES * nz, HALVES * nz)
        return lax.rem(z, nz) * CORES + c, aux_of(y, z // nz, x)

    def across(hops):
        return p, aux_of(y, half, lax.rem(x + hops + ROW, ROW))

    def along(hops):
        return p, aux_of(lax.rem(y + hops + ny, ny), half, x)

    def greet(semaphore, devices):
        for device in devices:
            pl.semaphore_signal(semaphore, inc=1, device_id=device, device_id_type=MESH)

    greet(barrier, [ring(1), ring(-1), (sib, j), across(1), across(-1), along(1), along(-1)])

    word = [
        [(word_sem.at[0], [across(1), across(-1)]), (word_sem.at[1], [ring(1), ring(-1)])],
        [(word_sem.at[2], [along(1), along(-1)]), (word_sem.at[3], [ring(2), ring(-2)])],
        [(word_sem.at[4], [along(1), along(-1)]), (word_sem.at[5], [ring(4), ring(-4)])],
    ]

    def pass_word(turn):
        if turn > 0:
            for semaphore, devices in word[turn - 1]:
                pl.semaphore_wait(semaphore, len(devices))
        if turn < len(word):
            for semaphore, devices in word[turn]:
                greet(semaphore, devices)

    load_i = pltpu.make_async_copy(ints_hbm, ibuf, local_sem.at[0])
    load_z = pltpu.make_async_copy(z_hbm, zbuf.at[p], local_sem.at[1])
    own_x = xchip.at[pl.ds(c * blocks_own, blocks_own)]
    load_x = pltpu.make_async_copy(x_hbm, own_x, local_sem.at[2])
    load_cols = pltpu.make_async_copy(cols_hbm, cols_ref, local_sem.at[3])
    load_live = pltpu.make_async_copy(live_hbm, live_ref, local_sem.at[4])
    load_x.start()
    load_cols.start()
    load_live.start()
    load_z.start()
    load_i.start()
    pl.semaphore_wait(barrier, 7)

    def z_copy(direction, shard_chip, piece, own=False):
        rows = pl.ds(pl.multiple_of(piece * piece_rows, piece_rows), piece_rows)
        shard = shard_chip * CORES + c
        src = z_hbm.at[rows] if own else zbuf.at[shard, rows]
        target = p + CORES if direction == 0 else p - CORES
        return pltpu.make_async_remote_copy(
            src_ref=src,
            dst_ref=zbuf.at[shard, rows],
            send_sem=z_send.at[direction, shard_chip, piece],
            recv_sem=z_recv.at[shard, piece],
            device_id=(target, j),
            device_id_type=MESH,
        )

    def z_side_copy(shard_chip, piece, own=False):
        rows = pl.ds(pl.multiple_of(piece * piece_rows, piece_rows), piece_rows)
        shard = shard_chip * CORES + c
        src = z_hbm.at[rows] if own else zbuf.at[shard, rows]
        return pltpu.make_async_remote_copy(
            src_ref=src,
            dst_ref=zbuf.at[shard, rows],
            send_sem=z_side.at[0],
            recv_sem=z_recv.at[shard, piece],
            device_id=(sib, j),
            device_id_type=MESH,
        )

    def z_arrived(shard, piece):
        rows = pl.ds(pl.multiple_of(piece * piece_rows, piece_rows), piece_rows)
        pltpu.make_async_copy(
            zbuf.at[shard, rows], zbuf.at[shard, rows], z_recv.at[shard, piece]
        ).wait()

    x_side = pltpu.make_async_remote_copy(
        src_ref=x_hbm,
        dst_ref=own_x,
        send_sem=xchip_send.at[0],
        recv_sem=xchip_recv.at[0],
        device_id=(sib, j),
        device_id_type=MESH,
    )
    x_side.start()
    for piece in range(PIECES):

        @pl.when(k < nz - 1)
        def _():
            z_copy(0, k, piece, own=True).start()

        @pl.when(k > 0)
        def _():
            z_copy(1, k, piece, own=True).start()

    for piece in range(PIECES):
        z_side_copy(k, piece, own=True).start()

    load_x.wait()
    load_cols.wait()
    load_live.wait()
    pltpu.make_async_copy(own_x, own_x, xchip_recv.at[0]).wait()

    def picked(dest, slot):
        number = (dest * CORES + c) * slots + slot
        local = cols_ref[number] - k * blocks_chip
        near = jnp.minimum(jnp.maximum(local, 0), blocks_chip - 1)
        here = (near == local).astype(jnp.float32)
        return xchip[near].astype(jnp.float32) * here

    def x_copy(direction, dest):
        target = p + CORES if direction == 0 else p - CORES
        return pltpu.make_async_remote_copy(
            src_ref=xout.at[dest],
            dst_ref=xin.at[direction, dest],
            send_sem=xr_send.at[direction, dest],
            recv_sem=xr_recv.at[direction, dest],
            device_id=(target, j),
            device_id_type=MESH,
        )

    def x_arrived(direction, dest):
        pltpu.make_async_copy(
            xin.at[direction, dest], xin.at[direction, dest], xr_recv.at[direction, dest]
        ).wait()

    def x_step(tau, _):
        for direction in range(2):
            place = k if direction == 0 else nz - 1 - k
            far = nz - 1 - tau + place
            dest = far if direction == 0 else nz - 1 - far

            @pl.when(place <= tau)
            def _():
                @pl.when(place > 0)
                def _():
                    x_arrived(direction, dest)
                    for slot in range(slots):
                        got = xin[direction, dest, slot].astype(jnp.float32)
                        xout[dest, slot] = (picked(dest, slot) + got).astype(xout.dtype)

                @pl.when(place == 0)
                def _():
                    for slot in range(slots):
                        xout[dest, slot] = picked(dest, slot).astype(xout.dtype)

                x_copy(direction, dest).start()

        return 0

    lead = min(LEAD, nz - 1)
    lax.fori_loop(0, lead, x_step, 0)

    x_peer = pltpu.make_async_remote_copy(
        src_ref=xout.at[k],
        dst_ref=xfull.at[y, half, x],
        send_sem=xpeer_send.at[0],
        recv_sem=xpeer_recv.at[0],
        device_id=(p, peer),
        device_id_type=MESH,
    )

    def x_last():
        for slot in range(slots):
            xout[k, slot] = picked(k, slot).astype(xout.dtype)

        @pl.when(k > 0)
        def _():
            x_arrived(0, k)
            for slot in range(slots):
                total = xout[k, slot].astype(jnp.float32) + xin[0, k, slot].astype(jnp.float32)
                xout[k, slot] = total.astype(xout.dtype)

        @pl.when(k < nz - 1)
        def _():
            x_arrived(1, k)
            for slot in range(slots):
                total = xout[k, slot].astype(jnp.float32) + xin[1, k, slot].astype(jnp.float32)
                xout[k, slot] = total.astype(xout.dtype)

        xfull[y, half, x] = xout[k]
        x_peer.start()

    def gathered(hh, kind):
        if kind == 0:
            return xfull.at[y, hh, x, 0], xfull.at[0, hh, pl.ds(0, ROW - 1), 0], across, ROW
        if kind == 1:
            return xfull.at[y, hh, x, 1], xfull.at[pl.ds(0, ny - 1), hh, 0, 1], along, ny
        if kind == 2:
            return xfull.at[y, hh, :, 0], xfull.at[pl.ds(0, ny - 1), hh, :, 0], along, ny
        return xfull.at[:, hh, x, 1], xfull.at[:, hh, pl.ds(0, ROW - 1), 1], across, ROW

    def x_gather(hh, stage, kind):
        block, _, line, length = gathered(hh, kind)
        for hops in range(1, length):
            pltpu.make_async_remote_copy(
                src_ref=block,
                dst_ref=block,
                send_sem=xg_send.at[stage, kind],
                recv_sem=xg_recv.at[stage, kind],
                device_id=line(hops),
                device_id_type=MESH,
            ).start()

    def x_gathered(stage, kind, semaphore):
        _, some, _, _ = gathered(0, kind)
        pltpu.make_async_copy(some, some, semaphore.at[stage, kind]).wait()

    def x_gather_on(hh, stage):
        for kind in range(2):
            x_gathered(stage, kind, xg_recv)
            x_gather(hh, stage, kind + 2)

    def x_plane_arrived(stage):
        for kind in range(2, 4):
            x_gathered(stage, kind, xg_recv)

    def multiply(shard):
        z = zbuf[shard]
        for slot in range(slots):
            prod[shard, slot] = lax.dot_general(
                ibuf[slot], z, (((1,), (1,)), ((), ())), preferred_element_type=jnp.float32
            )

    def contract(shard):
        for slot in range(slots):
            alive = live_ref[p * slots + slot].astype(jnp.float32)
            for h in range(chunks):
                chunk = shard * chunks + h
                yy, hh, xx = chunk // (HALVES * ROW), (chunk // ROW) % HALVES, chunk % ROW
                rows = xfull[yy, hh, xx, slot].astype(jnp.float32)
                part = prod[shard, slot, :, h * width : (h + 1) * width]
                part = part.reshape(mus, width, width)
                term = jnp.sum(part * rows[None], axis=1) * alive
                tpart[chunk, slot * mus : (slot + 1) * mus, :] = term
        for h in range(chunks):
            chunk = shard * chunks + h
            yy = chunk // (HALVES * ROW)
            hh = (chunk // ROW) % HALVES
            xx = chunk % ROW
            rel = lax.rem(y - yy + ny, ny) * ROW + lax.rem(x - xx + ROW, ROW)

            @pl.when(rel > 0)
            def _():
                pltpu.make_async_remote_copy(
                    src_ref=tpart.at[chunk],
                    dst_ref=trecv.at[hh, rel - 1],
                    send_sem=t1_send.at[0],
                    recv_sem=t1_recv.at[hh],
                    device_id=(p, aux_of(yy, half, xx)),
                    device_id_type=MESH,
                ).start()

    def for_set(step, first, last, what):
        def one(n, _):
            direction = n // CORES
            core = lax.rem(c + n, CORES)
            chip = jnp.where((direction == 0) == (k >= nz // 2), k - step, k + step)
            shard = chip * CORES + core
            valid = jnp.logical_and(chip >= 0, chip < nz)
            valid = jnp.logical_and(valid, jnp.logical_or(step > 0, direction == 0))

            @pl.when(valid)
            def _():
                what(shard, core)

            return 0

        lax.fori_loop(first, last, one, 0)

    def multiply_arrived(shard, core):
        @pl.when(core != c)
        def _():
            for piece in range(PIECES):
                z_arrived(shard, piece)

        multiply(shard)

    def contract_ready(shard, core):
        contract(shard)

    load_z.wait()
    load_i.wait()

    early = nz // 2 - 1
    ready = PIECES * (nz - 2)
    done_at = [ready] * early + [ready + 2] * (early + 1) + [PIECES * (nz - 1)]
    own_parity = lax.rem(half + k, 2)

    def step_of(item):
        own = own_parity + 2 * item
        other = 1 - own_parity + 2 * (item - early)
        return jnp.where(item < early, own, jnp.where(item < 2 * early, other, item))

    def item_of(step):
        own = lax.rem(step + own_parity, 2) == 0
        listed = jnp.where(own, (step - own_parity) // 2, early + (step - 1 + own_parity) // 2)
        return jnp.where(step < 2 * early, listed, step)

    def finished_at(item):
        event = jnp.int32(done_at[0])
        for n in range(1, nz):
            event = jnp.where(item >= n, done_at[n], event)
        return event

    def items_by(event):
        count = jnp.int32(0)
        for n in range(nz):
            count = count + (event >= done_at[n]).astype(jnp.int32)
        return count

    last_event = PIECES * (nz - 1) + 1
    x_event = X_EVERY * (nz - 1 - lead)
    shares = 2 * CORES // PIECES
    peer_event = min(x_event + PEER_LAG, done_at[early])

    def spread(hh):
        pltpu.make_async_copy(trecv.at[hh], trecv.at[hh], t1_recv.at[hh]).wait()
        sbuf[hh] = jnp.sum(trecv[hh], axis=0) + tpart[aux_of(y, hh, x)]
        near = jnp.where(half == hh, 1, 0)

        def send(rel, _):
            slot = jnp.where(half == hh, pairs - 1 - rel, pairs - 1 + lax.rem(pairs - rel, pairs))
            pltpu.make_async_remote_copy(
                src_ref=sbuf.at[hh],
                dst_ref=fin.at[slot],
                send_sem=t2_send.at[0],
                recv_sem=t2_recv.at[0],
                device_id=(lax.rem(p + rel, pairs), aux_of(y, hh, x)),
                device_id_type=MESH,
            ).start()
            return 0

        lax.fori_loop(near, pairs, send, 0)

    def event_step(event, _):
        t = event // PIECES + 1
        piece = lax.rem(event, PIECES)

        @pl.when(k - t >= 0)
        def _():
            z_arrived((k - t) * CORES + c, piece)

            @pl.when(k < nz - 1)
            def _():
                z_copy(0, k - t, piece).start()

            z_side_copy(k - t, piece).start()

        @pl.when(k + t < nz)
        def _():
            z_arrived((k + t) * CORES + c, piece)

            @pl.when(k > 0)
            def _():
                z_copy(1, k + t, piece).start()

            z_side_copy(k + t, piece).start()

        @pl.when(jnp.logical_and(event < x_event, lax.rem(event, X_EVERY) == 0))
        def _():
            x_step(event // X_EVERY + lead, 0)

        for turn, at in enumerate(WORD_EVENTS):

            @pl.when(event == min(at, x_event))
            def _():
                pass_word(turn)

        @pl.when(event == x_event)
        def _():
            x_last()
            x_gather(half, 0, 0)
            x_gather(half, 0, 1)

        @pl.when(event == peer_event)
        def _():
            pltpu.make_async_copy(xout.at[0], xout.at[0], xpeer_recv.at[0]).wait()
            x_gather(1 - half, 1, 0)
            x_gather(1 - half, 1, 1)

        @pl.when(event == min(x_event + ON_LAG, done_at[0]))
        def _():
            x_gather_on(half, 0)

        @pl.when(event == min(peer_event + ON_LAG, done_at[early]))
        def _():
            x_gather_on(1 - half, 1)

        @pl.when(event == done_at[0])
        def _():
            x_plane_arrived(0)

        @pl.when(event == done_at[early])
        def _():
            x_plane_arrived(1)

        for hh in range(HALVES):
            step = jnp.abs(k - aux_of(y, hh, x) // (chunks * CORES))

            @pl.when(event == jnp.minimum(finished_at(item_of(step)) + SUM_LAG, last_event))
            def _():
                spread(hh)

        ending = event == PIECES * (nz - 1)
        first = jnp.where(ending, 0, piece * shares)
        last = jnp.where(ending, 2 * CORES, (piece + 1) * shares)
        for_set(t - 1, first, jnp.where(event > PIECES * (nz - 1), 0, last), multiply_arrived)

        def work(item, _):
            for_set(step_of(item), 0, 2 * CORES, contract_ready)
            return 0

        lax.fori_loop(items_by(event - 1), items_by(event), work, 0)

        return 0

    lax.fori_loop(0, last_event + 1, event_step, 0)

    x_side.wait_send()
    x_peer.wait_send()
    pltpu.make_async_copy(trecv, trecv, t1_send.at[0]).wait()
    for stage in range(HALVES):
        for kind in range(4):
            x_gathered(stage, kind, xg_send)
    sent_z = zbuf.at[pl.ds(0, nz)]
    pltpu.make_async_copy(sent_z, sent_z, z_side.at[0]).wait()

    def z_sent(chip, _):
        @pl.when(jnp.logical_and(chip <= k, k < nz - 1))
        def _():
            for piece in range(PIECES):
                z_copy(0, chip, piece).wait_send()

        @pl.when(jnp.logical_and(chip >= k, k > 0))
        def _():
            for piece in range(PIECES):
                z_copy(1, chip, piece).wait_send()

        @pl.when(chip > k)
        def _():
            x_copy(0, chip).wait_send()

        @pl.when(chip < k)
        def _():
            x_copy(1, chip).wait_send()

        return 0

    lax.fori_loop(0, nz, z_sent, 0)

    pltpu.make_async_copy(fin, fin, t2_recv.at[0]).wait()
    out_ref[p] = sbuf[half] + fin[pairs - 1]

    def take(rel, _):
        out_ref[lax.rem(p + rel, pairs)] = fin[rel - 1] + fin[pairs - 1 + rel]
        return 0

    lax.fori_loop(1, pairs, take, 0)
    pltpu.make_async_copy(fin, fin, t2_send.at[0]).wait()


def place_kernel(first_block, blocks_dev, strips, slots, rows_ref, strip_ref, sums_ref, out_ref):
    out_ref[...] = jnp.zeros_like(out_ref)
    base = first_block[0]
    rows, columns = sums_ref.shape[1:]
    mus = rows // slots
    sublane = lax.broadcasted_iota(jnp.int32, (rows, columns), 0) // mus

    def body(p, _):
        value = sums_ref[p]
        turned = pltpu.roll(value, mus, 0)
        for slot in range(slots):
            number = p * slots + slot
            local = rows_ref[number] - base
            strip = local * strips + strip_ref[number]
            part = strip % slots
            tile = strip // slots

            @pl.when(jnp.logical_and(local >= 0, local < blocks_dev))
            def _():
                moved = jnp.where(part == slot, value, turned)
                kept = jnp.where(sublane == part, moved, 0.0)
                at = pl.ds(pl.multiple_of(tile * rows, rows), rows)
                out_ref[at, :] = out_ref[at, :] + kept

        return 0

    lax.fori_loop(0, sums_ref.shape[0], body, 0)


def per_device(
    integral_strips,
    slot_row_block,
    slot_strip_index,
    slot_column_block,
    block_live,
    ao_factor,
    aux_factor,
):
    slots, strip_size, depth = integral_strips.shape
    width = BLOCK_FUNCTIONS
    mus = strip_size // width
    pairs = lax.axis_size("pair")
    auxes = lax.axis_size("aux")
    nz = pairs // CORES
    plane = auxes // HALVES
    shard_rows = aux_factor.shape[0]
    rows_x, rank_part = ao_factor.shape
    blocks_dev = rows_x // width
    x_blocks = ao_factor.reshape(blocks_dev, width, rank_part)
    smem = pl.BlockSpec(memory_space=pltpu.SMEM)
    hbm = pl.BlockSpec(memory_space=pltpu.HBM)
    vmem = pl.BlockSpec(memory_space=pltpu.VMEM)
    rows = slots * mus
    dma = pltpu.SemaphoreType.DMA
    sums = pl.pallas_call(
        exchange_kernel,
        out_shape=jax.ShapeDtypeStruct((pairs, rows, rank_part), jnp.float32),
        in_specs=[hbm, hbm, hbm, hbm, hbm],
        out_specs=vmem,
        scratch_shapes=[
            pltpu.SMEM((slot_column_block.shape[0],), jnp.int32),
            pltpu.SMEM((block_live.shape[0],), jnp.int32),
            pltpu.VMEM((pairs, shard_rows, depth), jnp.bfloat16),
            pltpu.VMEM((slots, strip_size, depth), jnp.bfloat16),
            pltpu.VMEM((CORES * blocks_dev, width, rank_part), jnp.bfloat16),
            pltpu.VMEM((2, nz, slots, width, rank_part), jnp.bfloat16),
            pltpu.VMEM((nz, slots, width, rank_part), jnp.bfloat16),
            pltpu.VMEM((plane // ROW, HALVES, ROW, slots, width, rank_part), jnp.bfloat16),
            pltpu.VMEM((pairs, slots, strip_size, shard_rows), jnp.float32),
            pltpu.VMEM((auxes, rows, rank_part), jnp.float32),
            pltpu.VMEM((HALVES, plane - 1, rows, rank_part), jnp.float32),
            pltpu.VMEM((HALVES, rows, rank_part), jnp.float32),
            pltpu.VMEM((2 * pairs - 1, rows, rank_part), jnp.float32),
            dma((5,)),
            dma((2, nz, PIECES)),
            dma((1,)),
            dma((pairs, PIECES)),
            dma((1,)),
            dma((1,)),
            dma((2, nz)),
            dma((2, nz)),
            dma((1,)),
            dma((1,)),
            dma((HALVES, 4)),
            dma((HALVES, 4)),
            dma((1,)),
            dma((HALVES,)),
            dma((1,)),
            dma((1,)),
            pltpu.SemaphoreType.REGULAR((6,)),
        ],
        compiler_params=pltpu.CompilerParams(
            collective_id=0, has_side_effects=True, vmem_limit_bytes=60 * 2**20
        ),
        name="exchange",
    )(slot_column_block, block_live, integral_strips, x_blocks, aux_factor)

    first_block = (lax.axis_index("pair") * blocks_dev).astype(jnp.int32).reshape(1)
    return pl.pallas_call(
        lambda base, *refs: place_kernel(base, blocks_dev, width // mus, slots, *refs),
        out_shape=jax.ShapeDtypeStruct((rows_x, rank_part), jnp.float32),
        in_specs=[smem, smem, smem, vmem],
        out_specs=vmem,
        name="place",
    )(first_block, slot_row_block, slot_strip_index, sums)


def solution(mesh):
    in_specs = (P("pair", None, "aux"), P(), P(), P(), P(), P("pair", "aux"), P("pair", "aux"))
    out_specs = P("pair", "aux")
    return jax.shard_map(
        per_device, mesh=mesh, in_specs=in_specs, out_specs=out_specs, check_vma=False
    )
```

```python
import functools

import jax
import jax.numpy as jnp
from jax import lax
from jax.experimental import pallas as pl
from jax.experimental.pallas import tpu as pltpu
from jax.sharding import PartitionSpec as P

BLOCK_FUNCTIONS = 128
CORES = 2
HALVES = 2
ROW = 4
PIECES = 4
X_EVERY = PIECES // 2
LEAD = 0
PEER_LAG = 5
ON_LAG = 3
WORD_EVENTS = (0, 2, 5, 9)
SUM_LAG = 4
MESH = pl.DeviceIdType.MESH


def exchange_kernel(
    cols_hbm,
    live_hbm,
    ints_hbm,
    x_hbm,
    z_hbm,
    out_ref,
    cols_ref,
    live_ref,
    zbuf,
    ibuf,
    xchip,
    xin,
    xout,
    xfull,
    prod,
    tpart,
    trecv,
    sbuf,
    fin,
    local_sem,
    z_send,
    z_side,
    z_recv,
    xchip_send,
    xchip_recv,
    xr_send,
    xr_recv,
    xpeer_send,
    xpeer_recv,
    xg_send,
    xg_recv,
    t1_send,
    t1_recv,
    t2_send,
    t2_recv,
    word_sem,
):
    pairs = lax.axis_size("pair")
    auxes = lax.axis_size("aux")
    nz = pairs // CORES
    ny = auxes // (HALVES * ROW)
    plane = ny * ROW
    p = lax.axis_index("pair")
    j = lax.axis_index("aux")
    k = p // CORES
    c = p % CORES
    sib = p + 1 - 2 * c
    x = j % ROW
    half = (j // ROW) % HALVES
    y = j // (ROW * HALVES)
    peer = j + (1 - 2 * half) * ROW
    slots = ints_hbm.shape[0]
    blocks_own = x_hbm.shape[0]
    shard_rows = z_hbm.shape[0]
    piece_rows = shard_rows // PIECES
    chunks = shard_rows // BLOCK_FUNCTIONS
    width = BLOCK_FUNCTIONS
    mus = ints_hbm.shape[1] // width
    blocks_chip = CORES * blocks_own

    def aux_of(yy, hh, xx):
        return (yy * HALVES + hh) * ROW + xx

    def plane_aux(rel):
        return aux_of(lax.rem(y + rel // ROW, ny), half, lax.rem(x + rel % ROW, ROW))

    barrier = pltpu.get_barrier_semaphore()

    def ring(hops):
        z = lax.rem(half * nz + k + hops + HALVES * nz, HALVES * nz)
        return lax.rem(z, nz) * CORES + c, aux_of(y, z // nz, x)

    def across(hops):
        return p, aux_of(y, half, lax.rem(x + hops + ROW, ROW))

    def along(hops):
        return p, aux_of(lax.rem(y + hops + ny, ny), half, x)

    def greet(semaphore, devices):
        for device in devices:
            pl.semaphore_signal(semaphore, inc=1, device_id=device, device_id_type=MESH)

    greet(barrier, [ring(1), ring(-1), (sib, j), across(1), across(-1), along(1), along(-1)])

    word = [
        [(word_sem.at[0], [across(1), across(-1)]), (word_sem.at[1], [ring(1), ring(-1)])],
        [(word_sem.at[2], [along(1), along(-1)]), (word_sem.at[3], [ring(2), ring(-2)])],
        [(word_sem.at[4], [along(1), along(-1)]), (word_sem.at[5], [ring(4), ring(-4)])],
    ]

    def pass_word(turn):
        if turn > 0:
            for semaphore, devices in word[turn - 1]:
                pl.semaphore_wait(semaphore, len(devices))
        if turn < len(word):
            for semaphore, devices in word[turn]:
                greet(semaphore, devices)

    load_i = pltpu.make_async_copy(ints_hbm, ibuf, local_sem.at[0])
    load_z = pltpu.make_async_copy(z_hbm, zbuf.at[p], local_sem.at[1])
    own_x = xchip.at[pl.ds(c * blocks_own, blocks_own)]
    load_x = pltpu.make_async_copy(x_hbm, own_x, local_sem.at[2])
    load_cols = pltpu.make_async_copy(cols_hbm, cols_ref, local_sem.at[3])
    load_live = pltpu.make_async_copy(live_hbm, live_ref, local_sem.at[4])
    load_x.start()
    load_cols.start()
    load_live.start()
    load_z.start()
    load_i.start()
    pl.semaphore_wait(barrier, 7)

    def z_copy(direction, shard_chip, piece, own=False):
        rows = pl.ds(pl.multiple_of(piece * piece_rows, piece_rows), piece_rows)
        shard = shard_chip * CORES + c
        src = z_hbm.at[rows] if own else zbuf.at[shard, rows]
        target = p + CORES if direction == 0 else p - CORES
        return pltpu.make_async_remote_copy(
            src_ref=src,
            dst_ref=zbuf.at[shard, rows],
            send_sem=z_send.at[direction, shard_chip, piece],
            recv_sem=z_recv.at[shard, piece],
            device_id=(target, j),
            device_id_type=MESH,
        )

    def z_side_copy(shard_chip, piece, own=False):
        rows = pl.ds(pl.multiple_of(piece * piece_rows, piece_rows), piece_rows)
        shard = shard_chip * CORES + c
        src = z_hbm.at[rows] if own else zbuf.at[shard, rows]
        return pltpu.make_async_remote_copy(
            src_ref=src,
            dst_ref=zbuf.at[shard, rows],
            send_sem=z_side.at[0],
            recv_sem=z_recv.at[shard, piece],
            device_id=(sib, j),
            device_id_type=MESH,
        )

    def z_arrived(shard, piece):
        rows = pl.ds(pl.multiple_of(piece * piece_rows, piece_rows), piece_rows)
        pltpu.make_async_copy(
            zbuf.at[shard, rows], zbuf.at[shard, rows], z_recv.at[shard, piece]
        ).wait()

    x_side = pltpu.make_async_remote_copy(
        src_ref=x_hbm,
        dst_ref=own_x,
        send_sem=xchip_send.at[0],
        recv_sem=xchip_recv.at[0],
        device_id=(sib, j),
        device_id_type=MESH,
    )
    x_side.start()
    for piece in range(PIECES):

        @pl.when(k < nz - 1)
        def _():
            z_copy(0, k, piece, own=True).start()

        @pl.when(k > 0)
        def _():
            z_copy(1, k, piece, own=True).start()

    for piece in range(PIECES):
        z_side_copy(k, piece, own=True).start()

    load_x.wait()
    load_cols.wait()
    load_live.wait()
    pltpu.make_async_copy(own_x, own_x, xchip_recv.at[0]).wait()

    def picked(dest, slot):
        number = (dest * CORES + c) * slots + slot
        local = cols_ref[number] - k * blocks_chip
        near = jnp.minimum(jnp.maximum(local, 0), blocks_chip - 1)
        here = (near == local).astype(jnp.float32)
        return xchip[near].astype(jnp.float32) * here

    def x_copy(direction, dest):
        target = p + CORES if direction == 0 else p - CORES
        return pltpu.make_async_remote_copy(
            src_ref=xout.at[dest],
            dst_ref=xin.at[direction, dest],
            send_sem=xr_send.at[direction, dest],
            recv_sem=xr_recv.at[direction, dest],
            device_id=(target, j),
            device_id_type=MESH,
        )

    def x_arrived(direction, dest):
        pltpu.make_async_copy(
            xin.at[direction, dest], xin.at[direction, dest], xr_recv.at[direction, dest]
        ).wait()

    def x_step(tau, _):
        for direction in range(2):
            place = k if direction == 0 else nz - 1 - k
            far = nz - 1 - tau + place
            dest = far if direction == 0 else nz - 1 - far

            @pl.when(place <= tau)
            def _():
                @pl.when(place > 0)
                def _():
                    x_arrived(direction, dest)
                    for slot in range(slots):
                        got = xin[direction, dest, slot].astype(jnp.float32)
                        xout[dest, slot] = (picked(dest, slot) + got).astype(xout.dtype)

                @pl.when(place == 0)
                def _():
                    for slot in range(slots):
                        xout[dest, slot] = picked(dest, slot).astype(xout.dtype)

                x_copy(direction, dest).start()

        return 0

    lead = min(LEAD, nz - 1)
    lax.fori_loop(0, lead, x_step, 0)

    x_peer = pltpu.make_async_remote_copy(
        src_ref=xout.at[k],
        dst_ref=xfull.at[y, half, x],
        send_sem=xpeer_send.at[0],
        recv_sem=xpeer_recv.at[0],
        device_id=(p, peer),
        device_id_type=MESH,
    )

    def x_last():
        for slot in range(slots):
            xout[k, slot] = picked(k, slot).astype(xout.dtype)

        @pl.when(k > 0)
        def _():
            x_arrived(0, k)
            for slot in range(slots):
                total = xout[k, slot].astype(jnp.float32) + xin[0, k, slot].astype(jnp.float32)
                xout[k, slot] = total.astype(xout.dtype)

        @pl.when(k < nz - 1)
        def _():
            x_arrived(1, k)
            for slot in range(slots):
                total = xout[k, slot].astype(jnp.float32) + xin[1, k, slot].astype(jnp.float32)
                xout[k, slot] = total.astype(xout.dtype)

        xfull[y, half, x] = xout[k]
        x_peer.start()

    def gathered(hh, kind):
        if kind == 0:
            return xfull.at[y, hh, x, 0], xfull.at[0, hh, pl.ds(0, ROW - 1), 0], across, ROW
        if kind == 1:
            return xfull.at[y, hh, x, 1], xfull.at[pl.ds(0, ny - 1), hh, 0, 1], along, ny
        if kind == 2:
            return xfull.at[y, hh, :, 0], xfull.at[pl.ds(0, ny - 1), hh, :, 0], along, ny
        return xfull.at[:, hh, x, 1], xfull.at[:, hh, pl.ds(0, ROW - 1), 1], across, ROW

    def x_gather(hh, stage, kind):
        block, _, line, length = gathered(hh, kind)
        for hops in range(1, length):
            pltpu.make_async_remote_copy(
                src_ref=block,
                dst_ref=block,
                send_sem=xg_send.at[stage, kind],
                recv_sem=xg_recv.at[stage, kind],
                device_id=line(hops),
                device_id_type=MESH,
            ).start()

    def x_gathered(stage, kind, semaphore):
        _, some, _, _ = gathered(0, kind)
        pltpu.make_async_copy(some, some, semaphore.at[stage, kind]).wait()

    def x_gather_on(hh, stage):
        for kind in range(2):
            x_gathered(stage, kind, xg_recv)
            x_gather(hh, stage, kind + 2)

    def x_plane_arrived(stage):
        for kind in range(2, 4):
            x_gathered(stage, kind, xg_recv)

    def multiply(shard):
        z = zbuf[shard]
        for slot in range(slots):
            prod[shard, slot] = lax.dot_general(
                ibuf[slot], z, (((1,), (1,)), ((), ())), preferred_element_type=jnp.float32
            )

    def contract(shard):
        for slot in range(slots):
            alive = live_ref[p * slots + slot].astype(jnp.float32)
            for h in range(chunks):
                chunk = shard * chunks + h
                yy, hh, xx = chunk // (HALVES * ROW), (chunk // ROW) % HALVES, chunk % ROW
                rows = xfull[yy, hh, xx, slot].astype(jnp.float32)
                part = prod[shard, slot, :, h * width : (h + 1) * width]
                part = part.reshape(mus, width, width)
                term = jnp.sum(part * rows[None], axis=1) * alive
                tpart[chunk, slot * mus : (slot + 1) * mus, :] = term
        for h in range(chunks):
            chunk = shard * chunks + h
            yy = chunk // (HALVES * ROW)
            hh = (chunk // ROW) % HALVES
            xx = chunk % ROW
            rel = lax.rem(y - yy + ny, ny) * ROW + lax.rem(x - xx + ROW, ROW)

            @pl.when(rel > 0)
            def _():
                pltpu.make_async_remote_copy(
                    src_ref=tpart.at[chunk],
                    dst_ref=trecv.at[hh, rel - 1],
                    send_sem=t1_send.at[0],
                    recv_sem=t1_recv.at[hh],
                    device_id=(p, aux_of(yy, half, xx)),
                    device_id_type=MESH,
                ).start()

    def for_set(step, first, last, what):
        def one(n, _):
            direction = n // CORES
            core = lax.rem(c + n, CORES)
            chip = jnp.where((direction == 0) == (k >= nz // 2), k - step, k + step)
            shard = chip * CORES + core
            valid = jnp.logical_and(chip >= 0, chip < nz)
            valid = jnp.logical_and(valid, jnp.logical_or(step > 0, direction == 0))

            @pl.when(valid)
            def _():
                what(shard, core)

            return 0

        lax.fori_loop(first, last, one, 0)

    def multiply_arrived(shard, core):
        @pl.when(core != c)
        def _():
            for piece in range(PIECES):
                z_arrived(shard, piece)

        multiply(shard)

    def contract_ready(shard, core):
        contract(shard)

    load_z.wait()
    load_i.wait()

    early = nz // 2 - 1
    ready = PIECES * (nz - 2)
    done_at = [ready] * early + [ready + 2] * (early + 1) + [PIECES * (nz - 1)]
    own_parity = lax.rem(half + k, 2)

    def step_of(item):
        own = own_parity + 2 * item
        other = 1 - own_parity + 2 * (item - early)
        return jnp.where(item < early, own, jnp.where(item < 2 * early, other, item))

    def item_of(step):
        own = lax.rem(step + own_parity, 2) == 0
        listed = jnp.where(own, (step - own_parity) // 2, early + (step - 1 + own_parity) // 2)
        return jnp.where(step < 2 * early, listed, step)

    def finished_at(item):
        event = jnp.int32(done_at[0])
        for n in range(1, nz):
            event = jnp.where(item >= n, done_at[n], event)
        return event

    def items_by(event):
        count = jnp.int32(0)
        for n in range(nz):
            count = count + (event >= done_at[n]).astype(jnp.int32)
        return count

    last_event = PIECES * (nz - 1) + 1
    x_event = X_EVERY * (nz - 1 - lead)
    shares = 2 * CORES // PIECES
    peer_event = min(x_event + PEER_LAG, done_at[early])

    def spread(hh):
        pltpu.make_async_copy(trecv.at[hh], trecv.at[hh], t1_recv.at[hh]).wait()
        sbuf[hh] = jnp.sum(trecv[hh], axis=0) + tpart[aux_of(y, hh, x)]
        near = jnp.where(half == hh, 1, 0)

        def send(rel, _):
            slot = jnp.where(half == hh, pairs - 1 - rel, pairs - 1 + lax.rem(pairs - rel, pairs))
            pltpu.make_async_remote_copy(
                src_ref=sbuf.at[hh],
                dst_ref=fin.at[slot],
                send_sem=t2_send.at[0],
                recv_sem=t2_recv.at[0],
                device_id=(lax.rem(p + rel, pairs), aux_of(y, hh, x)),
                device_id_type=MESH,
            ).start()
            return 0

        lax.fori_loop(near, pairs, send, 0)

    def event_step(event, _):
        t = event // PIECES + 1
        piece = lax.rem(event, PIECES)

        @pl.when(k - t >= 0)
        def _():
            z_arrived((k - t) * CORES + c, piece)

            @pl.when(k < nz - 1)
            def _():
                z_copy(0, k - t, piece).start()

            z_side_copy(k - t, piece).start()

        @pl.when(k + t < nz)
        def _():
            z_arrived((k + t) * CORES + c, piece)

            @pl.when(k > 0)
            def _():
                z_copy(1, k + t, piece).start()

            z_side_copy(k + t, piece).start()

        @pl.when(jnp.logical_and(event < x_event, lax.rem(event, X_EVERY) == 0))
        def _():
            x_step(event // X_EVERY + lead, 0)

        for turn, at in enumerate(WORD_EVENTS):

            @pl.when(event == min(at, x_event))
            def _():
                pass_word(turn)

        @pl.when(event == x_event)
        def _():
            x_last()
            x_gather(half, 0, 0)
            x_gather(half, 0, 1)

        @pl.when(event == peer_event)
        def _():
            pltpu.make_async_copy(xout.at[0], xout.at[0], xpeer_recv.at[0]).wait()
            x_gather(1 - half, 1, 0)
            x_gather(1 - half, 1, 1)

        @pl.when(event == min(x_event + ON_LAG, done_at[0]))
        def _():
            x_gather_on(half, 0)

        @pl.when(event == min(peer_event + ON_LAG, done_at[early]))
        def _():
            x_gather_on(1 - half, 1)

        @pl.when(event == done_at[0])
        def _():
            x_plane_arrived(0)

        @pl.when(event == done_at[early])
        def _():
            x_plane_arrived(1)

        for hh in (1 - half, half):
            step = jnp.abs(k - aux_of(y, hh, x) // (chunks * CORES))

            @pl.when(event == jnp.minimum(finished_at(item_of(step)) + SUM_LAG, last_event))
            def _():
                spread(hh)

        ending = event == PIECES * (nz - 1)
        first = jnp.where(ending, 0, piece * shares)
        last = jnp.where(ending, 2 * CORES, (piece + 1) * shares)
        for_set(t - 1, first, jnp.where(event > PIECES * (nz - 1), 0, last), multiply_arrived)

        def work(item, _):
            for_set(step_of(item), 0, 2 * CORES, contract_ready)
            return 0

        lax.fori_loop(items_by(event - 1), items_by(event), work, 0)

        return 0

    lax.fori_loop(0, last_event + 1, event_step, 0)

    x_side.wait_send()
    x_peer.wait_send()
    pltpu.make_async_copy(trecv, trecv, t1_send.at[0]).wait()
    for stage in range(HALVES):
        for kind in range(4):
            x_gathered(stage, kind, xg_send)
    sent_z = zbuf.at[pl.ds(0, nz)]
    pltpu.make_async_copy(sent_z, sent_z, z_side.at[0]).wait()

    def z_sent(chip, _):
        @pl.when(jnp.logical_and(chip <= k, k < nz - 1))
        def _():
            for piece in range(PIECES):
                z_copy(0, chip, piece).wait_send()

        @pl.when(jnp.logical_and(chip >= k, k > 0))
        def _():
            for piece in range(PIECES):
                z_copy(1, chip, piece).wait_send()

        @pl.when(chip > k)
        def _():
            x_copy(0, chip).wait_send()

        @pl.when(chip < k)
        def _():
            x_copy(1, chip).wait_send()

        return 0

    lax.fori_loop(0, nz, z_sent, 0)

    pltpu.make_async_copy(fin, fin, t2_recv.at[0]).wait()
    out_ref[p] = sbuf[half] + fin[pairs - 1]

    def take(rel, _):
        out_ref[lax.rem(p + rel, pairs)] = fin[rel - 1] + fin[pairs - 1 + rel]
        return 0

    lax.fori_loop(1, pairs, take, 0)
    pltpu.make_async_copy(fin, fin, t2_send.at[0]).wait()


def place_kernel(first_block, blocks_dev, strips, slots, rows_ref, strip_ref, sums_ref, out_ref):
    out_ref[...] = jnp.zeros_like(out_ref)
    base = first_block[0]
    rows, columns = sums_ref.shape[1:]
    mus = rows // slots
    sublane = lax.broadcasted_iota(jnp.int32, (rows, columns), 0) // mus

    def body(p, _):
        value = sums_ref[p]
        turned = pltpu.roll(value, mus, 0)
        for slot in range(slots):
            number = p * slots + slot
            local = rows_ref[number] - base
            strip = local * strips + strip_ref[number]
            part = strip % slots
            tile = strip // slots

            @pl.when(jnp.logical_and(local >= 0, local < blocks_dev))
            def _():
                moved = jnp.where(part == slot, value, turned)
                kept = jnp.where(sublane == part, moved, 0.0)
                at = pl.ds(pl.multiple_of(tile * rows, rows), rows)
                out_ref[at, :] = out_ref[at, :] + kept

        return 0

    lax.fori_loop(0, sums_ref.shape[0], body, 0)


def per_device(
    integral_strips,
    slot_row_block,
    slot_strip_index,
    slot_column_block,
    block_live,
    ao_factor,
    aux_factor,
):
    slots, strip_size, depth = integral_strips.shape
    width = BLOCK_FUNCTIONS
    mus = strip_size // width
    pairs = lax.axis_size("pair")
    auxes = lax.axis_size("aux")
    nz = pairs // CORES
    plane = auxes // HALVES
    shard_rows = aux_factor.shape[0]
    rows_x, rank_part = ao_factor.shape
    blocks_dev = rows_x // width
    x_blocks = ao_factor.reshape(blocks_dev, width, rank_part)
    smem = pl.BlockSpec(memory_space=pltpu.SMEM)
    hbm = pl.BlockSpec(memory_space=pltpu.HBM)
    vmem = pl.BlockSpec(memory_space=pltpu.VMEM)
    rows = slots * mus
    dma = pltpu.SemaphoreType.DMA
    sums = pl.pallas_call(
        exchange_kernel,
        out_shape=jax.ShapeDtypeStruct((pairs, rows, rank_part), jnp.float32),
        in_specs=[hbm, hbm, hbm, hbm, hbm],
        out_specs=vmem,
        scratch_shapes=[
            pltpu.SMEM((slot_column_block.shape[0],), jnp.int32),
            pltpu.SMEM((block_live.shape[0],), jnp.int32),
            pltpu.VMEM((pairs, shard_rows, depth), jnp.bfloat16),
            pltpu.VMEM((slots, strip_size, depth), jnp.bfloat16),
            pltpu.VMEM((CORES * blocks_dev, width, rank_part), jnp.bfloat16),
            pltpu.VMEM((2, nz, slots, width, rank_part), jnp.bfloat16),
            pltpu.VMEM((nz, slots, width, rank_part), jnp.bfloat16),
            pltpu.VMEM((plane // ROW, HALVES, ROW, slots, width, rank_part), jnp.bfloat16),
            pltpu.VMEM((pairs, slots, strip_size, shard_rows), jnp.float32),
            pltpu.VMEM((auxes, rows, rank_part), jnp.float32),
            pltpu.VMEM((HALVES, plane - 1, rows, rank_part), jnp.float32),
            pltpu.VMEM((HALVES, rows, rank_part), jnp.float32),
            pltpu.VMEM((2 * pairs - 1, rows, rank_part), jnp.float32),
            dma((5,)),
            dma((2, nz, PIECES)),
            dma((1,)),
            dma((pairs, PIECES)),
            dma((1,)),
            dma((1,)),
            dma((2, nz)),
            dma((2, nz)),
            dma((1,)),
            dma((1,)),
            dma((HALVES, 4)),
            dma((HALVES, 4)),
            dma((1,)),
            dma((HALVES,)),
            dma((1,)),
            dma((1,)),
            pltpu.SemaphoreType.REGULAR((6,)),
        ],
        compiler_params=pltpu.CompilerParams(
            collective_id=0, has_side_effects=True, vmem_limit_bytes=60 * 2**20
        ),
        name="exchange",
    )(slot_column_block, block_live, integral_strips, x_blocks, aux_factor)

    first_block = (lax.axis_index("pair") * blocks_dev).astype(jnp.int32).reshape(1)
    return pl.pallas_call(
        lambda base, *refs: place_kernel(base, blocks_dev, width // mus, slots, *refs),
        out_shape=jax.ShapeDtypeStruct((rows_x, rank_part), jnp.float32),
        in_specs=[smem, smem, smem, vmem],
        out_specs=vmem,
        name="place",
    )(first_block, slot_row_block, slot_strip_index, sums)


def solution(mesh):
    in_specs = (P("pair", None, "aux"), P(), P(), P(), P(), P("pair", "aux"), P("pair", "aux"))
    out_specs = P("pair", "aux")
    return jax.shard_map(
        per_device, mesh=mesh, in_specs=in_specs, out_specs=out_specs, check_vma=False
    )
```
